512 devices in a mesh: seq: 32 (over z, core), head: 16 (over x, y).
Axes of the slice: x: 4, y: 4, z: 16, core: 2. Of those that a mesh axis runs over, the one named last changes fastest.
Arguments:
- queries: bfloat16 [12288, 12288], P('seq', 'head'), may hold values from -2.5 to 2.5
- key_states: bfloat16 [12288, 1024], P('seq'), may hold values from -2.5 to 2.5
- value_states: bfloat16 [12288, 1024], P('seq'), may hold values from -4 to 4
- attn_out: bfloat16 [12288, 12288], P('seq', 'head'), may hold values from -4 to 4
- grad_out: bfloat16 [12288, 12288], P('seq', 'head'), may hold values from -4 to 4
- log_norm: bfloat16 [96, 12288], P('head', 'seq'), may hold values from 0.1 to 9
- lengths: int32 [30], replicated, may hold values from 1 to 1153, as said below
- block_plan: int32 [96], replicated, may hold values from 0 to 95, as said below
Outputs:
- query_grad: bfloat16 [12288, 12288], P('seq', 'head')
- key_grad: bfloat16 [12288, 1024], P('seq', 'head')
- value_grad: bfloat16 [12288, 1024], P('seq', 'head')
The draws below stay inside these ranges and needn't reach their ends.
Inputs may be any that keep to these rules, and one draw needn't show every extreme that they name: The documents' lengths in their order along the sequence; they sum to 12288, and exactly one of them has 1153 tokens. `block_plan`: a permutation of the 96 blocks of 128 query tokens; slot s belongs to the device of index s // 3 along seq and names a block that lies on that device or on the device half the axis away.
All inputs are finite; a program needn't handle non-finite values.
Results may differ from the reference program's by a relative error of at most 0.015.
Values may be sent and summed in bfloat16 or wider, within the bound.
No kernel may reach another device: no remote copies, remote signals or barrier semaphores. Data moves between devices by JAX's collectives and lax.ppermute only.
A program may use at most 128 MiB of HBM per device.

```python
import jax
import jax.numpy as jnp
from jax import lax

HEAD_DIM = 128
TOK_DEV = 384
BLOCK = 128
HEADS = 96
KV_HEADS = 8
TOKENS = 12288
BLOCKS = 96
MOST = 1153
DOCS = 30
N_SEQ = 32


def document_lengths(key):
    own_key = jax.random.fold_in(key, 101)
    weight_key, place_key = jax.random.split(own_key)
    others = DOCS - 1
    remaining = TOKENS - MOST
    weights = jax.random.randint(weight_key, (others,), 4, 13, dtype=jnp.int32)
    shares = weights * remaining // jnp.sum(weights)
    leftover = remaining - jnp.sum(shares)
    shares = shares + (jnp.arange(others, dtype=jnp.int32) < leftover).astype(jnp.int32)
    longest_at = jax.random.randint(place_key, (), 0, DOCS, dtype=jnp.int32)
    places = jnp.arange(DOCS, dtype=jnp.int32)
    source = jnp.clip(jnp.where(places < longest_at, places, places - 1), 0, others - 1)
    return jnp.where(places == longest_at, MOST, shares[source]).astype(jnp.int32)


def token_counts(lengths):
    doc_ends = jnp.cumsum(lengths).astype(jnp.int32)
    positions = jnp.arange(TOKENS, dtype=jnp.int32)
    owner_doc = jnp.sum((positions[:, None] >= doc_ends[None, :]).astype(jnp.int32), axis=1)
    begins = jnp.concatenate([jnp.zeros((1,), jnp.int32), doc_ends])[owner_doc]
    return positions - begins + 1


def draw_lengths(key, part):
    lengths = document_lengths(key)
    return lengths


def draw_block_plan(key, part):
    lengths = document_lengths(key)
    key = jax.random.fold_in(key, 7)
    per_device = TOK_DEV // BLOCK
    devices = TOKENS // TOK_DEV
    half_devices = devices // 2
    block_cost = token_counts(lengths).reshape(TOKENS // BLOCK, BLOCK).sum(axis=1)
    lower_blocks = jnp.arange(half_devices, dtype=jnp.int32)[:, None] * per_device + jnp.arange(per_device, dtype=jnp.int32)[None, :]
    members = jnp.concatenate([lower_blocks, lower_blocks + half_devices * per_device], axis=1)
    within = jnp.arange(2 * per_device, dtype=jnp.int32)
    ranking_score = block_cost[members] * (2 * per_device) + within[None, :]
    rank_order = jnp.argsort(-ranking_score, axis=1)
    ranked = jnp.take_along_axis(members, rank_order, axis=1)
    first_ranks = [slot_rank for slot_rank in range(2 * per_device) if slot_rank % 4 in (0, 3)]
    second_ranks = [slot_rank for slot_rank in range(2 * per_device) if slot_rank % 4 in (1, 2)]
    first_set = ranked[:, jnp.array(first_ranks, dtype=jnp.int32)]
    second_set = ranked[:, jnp.array(second_ranks, dtype=jnp.int32)]
    flip_side = jax.random.randint(key, (half_devices, 1), 0, 2, dtype=jnp.int32)
    lower_slots = jnp.where(flip_side == 1, second_set, first_set)
    upper_slots = jnp.where(flip_side == 1, first_set, second_set)
    return jnp.concatenate([lower_slots.reshape(-1), upper_slots.reshape(-1)]).astype(jnp.int32)


def draw_log_norm(key, part):
    lengths = document_lengths(key)
    key = jax.random.fold_in(key, 11)
    counts = token_counts(lengths).astype(jnp.float32)
    offset = 0.7 + 0.5 * jax.random.uniform(key, (HEADS, TOKENS), jnp.float32, -1.0, 1.0)
    return (jnp.log(counts)[None, :] + offset).astype(jnp.bfloat16)


def steps_of(rng, shape, cuts, smallest, top_value):
    def one(position, parts):
        steps = jax.random.uniform(jax.random.fold_in(jax.random.fold_in(rng, 6), position), (parts,), jnp.float32, smallest / len(cuts), top_value / len(cuts))
        return jnp.repeat(jnp.exp(steps), shape[position] // parts).reshape((-1,) + (1,) * (len(shape) - position - 1))

    gain = one(*cuts[0])
    for cut in cuts[1:]:
        gain = gain * one(*cut)
    return gain


def normal_values(stream_key, dims, scale, most, pieces=(), kind=jnp.bfloat16):
    entries = scale * jax.random.normal(stream_key, dims, jnp.float32)
    if pieces:
        entries = entries * steps_of(stream_key, dims, pieces, -0.22, 0.18)
    return jnp.clip(entries, -most, most).astype(kind)


def setup_inputs(seed: int = 0) -> dict:
    seeds = jax.random.split(jax.random.key(seed), 9)
    queries = normal_values(seeds[0], (TOKENS, HEADS * HEAD_DIM), 1.0, 2.5, ((0, 32), (1, 16)))
    key_states = normal_values(seeds[1], (TOKENS, KV_HEADS * HEAD_DIM), 1.0, 2.5, ((0, 32),))
    value_states = normal_values(seeds[2], (TOKENS, KV_HEADS * HEAD_DIM), 1.0, 4.0, ((0, 32),))
    attn_out = normal_values(seeds[3], (TOKENS, HEADS * HEAD_DIM), 1.0, 4.0, ((0, 32), (1, 16)))
    grad_out = normal_values(seeds[4], (TOKENS, HEADS * HEAD_DIM), 1.0, 4.0, ((0, 32), (1, 16)))
    log_norm = draw_log_norm(jax.random.fold_in(seeds[8], 71), 0)
    lengths = draw_lengths(jax.random.fold_in(seeds[8], 71), 0)
    block_plan = draw_block_plan(jax.random.fold_in(seeds[8], 71), 0)
    return dict(queries=queries, key_states=key_states, value_states=value_states, attn_out=attn_out, grad_out=grad_out, log_norm=log_norm, lengths=lengths, block_plan=block_plan)


def doc_index(positions, doc_ends):
    return jnp.sum((positions[:, None] >= doc_ends[None, :]).astype(jnp.int32), axis=1)


def reference(queries, key_states, value_states, attn_out, grad_out, log_norm, lengths, block_plan):
    scaling = HEAD_DIM ** -0.5
    group_size = HEADS // KV_HEADS
    reach_rows = 3 * TOK_DEV
    window_rows = 4 * TOK_DEV
    doc_ends = jnp.cumsum(lengths).astype(jnp.int32)
    shape_five = (N_SEQ, TOK_DEV, KV_HEADS, group_size, HEAD_DIM)
    query_parts = queries.astype(jnp.float32).reshape(shape_five)
    outgrad_parts = grad_out.astype(jnp.float32).reshape(shape_five)
    row_delta = jnp.sum(outgrad_parts * attn_out.astype(jnp.float32).reshape(shape_five), axis=4)
    row_delta = row_delta.transpose(0, 2, 3, 1)
    norm_parts = log_norm.astype(jnp.float32).reshape(KV_HEADS, group_size, N_SEQ, TOK_DEV).transpose(2, 0, 1, 3)
    padding = jnp.zeros((reach_rows, KV_HEADS, HEAD_DIM), jnp.float32)
    keys_padded = jnp.concatenate([padding, key_states.astype(jnp.float32).reshape(TOKENS, KV_HEADS, HEAD_DIM)], axis=0)
    values_padded = jnp.concatenate([padding, value_states.astype(jnp.float32).reshape(TOKENS, KV_HEADS, HEAD_DIM)], axis=0)

    def part_step(running, inputs):
        key_acc, value_acc = running
        part_index, query_part, outgrad_part, delta_part, norm_part = inputs
        first_row = (part_index * TOK_DEV).astype(jnp.int32)
        key_rows = lax.dynamic_slice_in_dim(keys_padded, first_row, window_rows, 0)
        value_rows = lax.dynamic_slice_in_dim(values_padded, first_row, window_rows, 0)
        query_pos = first_row + jnp.arange(TOK_DEV, dtype=jnp.int32)
        key_pos = first_row - reach_rows + jnp.arange(window_rows, dtype=jnp.int32)
        allowed = ((doc_index(query_pos, doc_ends)[:, None] == doc_index(key_pos, doc_ends)[None, :])
                   & (key_pos[None, :] <= query_pos[:, None]) & (key_pos[None, :] >= 0))
        scores = jnp.einsum("qgjd,kgd->gjqk", query_part, key_rows, precision=lax.Precision.HIGHEST) * scaling
        weights = jnp.where(allowed, jnp.exp(scores - norm_part[:, :, :, None]), 0.0)
        weights_half = lax.optimization_barrier(weights.astype(jnp.bfloat16)).astype(jnp.float32)
        prob_grad = jnp.einsum("qgjd,kgd->gjqk", outgrad_part, value_rows, precision=lax.Precision.HIGHEST)
        score_grad = (weights * (prob_grad - delta_part[:, :, :, None])).astype(jnp.bfloat16)
        score_grad = lax.optimization_barrier(score_grad).astype(jnp.float32)
        query_grad = jnp.einsum("gjqk,kgd->qgjd", score_grad, key_rows, precision=lax.Precision.HIGHEST) * scaling
        key_grad = jnp.einsum("gjqk,qgjd->kgd", score_grad, query_part, precision=lax.Precision.HIGHEST) * scaling
        value_grad = jnp.einsum("gjqk,qgjd->kgd", weights_half, outgrad_part, precision=lax.Precision.HIGHEST)
        key_acc = lax.dynamic_update_slice_in_dim(
            key_acc, lax.dynamic_slice_in_dim(key_acc, first_row, window_rows, 0) + key_grad, first_row, 0)
        value_acc = lax.dynamic_update_slice_in_dim(
            value_acc, lax.dynamic_slice_in_dim(value_acc, first_row, window_rows, 0) + value_grad, first_row, 0)
        return (key_acc, value_acc), query_grad

    initial = (jnp.zeros_like(keys_padded), jnp.zeros_like(values_padded))
    part_indices = jnp.arange(N_SEQ, dtype=jnp.int32)
    (key_acc, value_acc), query_all = lax.scan(
        part_step, initial, (part_indices, query_parts, outgrad_parts, row_delta, norm_parts))
    full_query = query_all.reshape(TOKENS, HEADS * HEAD_DIM).astype(jnp.bfloat16)
    query_grad = full_query.reshape(BLOCKS, BLOCK, HEADS * HEAD_DIM)[block_plan].reshape(TOKENS, HEADS * HEAD_DIM)
    key_grad = key_acc[reach_rows:].reshape(TOKENS, KV_HEADS * HEAD_DIM).astype(jnp.bfloat16)
    value_grad = value_acc[reach_rows:].reshape(TOKENS, KV_HEADS * HEAD_DIM).astype(jnp.bfloat16)
    return (query_grad, key_grad, value_grad)
```

```python
import functools

import jax
import jax.numpy as jnp
from jax import lax
from jax.experimental import pallas as pl
from jax.experimental.pallas import tpu as pltpu
from jax.sharding import PartitionSpec as P

HEAD_DIM = 128
BLOCK = 128
BACK = 3
LOG2E = 1.4426950408889634
SCALE = HEAD_DIM ** -0.5


def shifted(value, axis, steps):
    count = lax.axis_size(axis)
    first, last = (max(0, -steps), min(count, count - steps))
    return lax.ppermute(value, axis, [(i, i + steps) for i in range(first, last)])


def swapped(array, axis, apart):
    return lax.ppermute(array, axis, [(i, i ^ apart) for i in range(lax.axis_size(axis))])


def dot(a, b):
    return jnp.dot(a, b, preferred_element_type=jnp.float32)


def dot_nt(a, b):
    return lax.dot_general(a, b, (((1,), (1,)), ((), ())), preferred_element_type=jnp.float32)


def stack_heads(wide_ref, stacked_ref, heads):
    for h in range(heads):
        stacked_ref[pl.ds(h * HEAD_DIM, HEAD_DIM), :] = wide_ref[:, pl.ds(h * HEAD_DIM, HEAD_DIM)]


def tile_grads(kt, vt, qs_ref, dos_ref, lse_ref, delta_ref, allowed, heads):
    scores = dot_nt(kt, qs_ref[...])
    prob_grad = dot_nt(vt, dos_ref[...])
    weights, score_grads = [], []
    for h in range(heads):
        cols = slice(h * BLOCK, (h + 1) * BLOCK)
        lse = lse_ref[h : h + 1, :].astype(jnp.float32) * LOG2E
        w = jnp.where(allowed, jnp.exp2(scores[:, cols] * (SCALE * LOG2E) - lse), 0.0)
        weights.append(w.astype(jnp.bfloat16))
        score_grads.append((w * (prob_grad[:, cols] - delta_ref[h : h + 1, :])).astype(jnp.bfloat16))
    w_half = jnp.concatenate(weights, axis=1)
    s_grad = jnp.concatenate(score_grads, axis=1)
    dv = dot(w_half, dos_ref[...])
    dk = dot(s_grad, qs_ref[...])
    dq_t = dot(kt.T, s_grad)
    return dq_t, dk, dv


def own_kernel(heads, starts_ref, pos_ref, kv_ref, q_ref, o_ref, do_ref, lse_ref,
               dq_ref, dkv_ref, delta_ref, qs_ref, dos_ref):
    j = pl.program_id(0)

    @pl.when(j == 0)
    def _():
        dkv_ref[...] = jnp.zeros_like(dkv_ref)

    stack_heads(q_ref, qs_ref, heads)
    stack_heads(do_ref, dos_ref, heads)
    ones = jnp.ones((8, 2 * HEAD_DIM), jnp.bfloat16)
    for h in range(heads):
        cols = pl.ds(h * HEAD_DIM, HEAD_DIM)
        prod = do_ref[:, cols].astype(jnp.float32) * o_ref[:, cols].astype(jnp.float32)
        high = prod.astype(jnp.bfloat16)
        low = (prod - high.astype(jnp.float32)).astype(jnp.bfloat16)
        row = dot_nt(ones, jnp.concatenate([high, low], axis=1))
        delta_ref[h : h + 1, :] = row[0:1, :]
    dq_ref[...] = jnp.zeros_like(dq_ref)
    start_row = starts_ref[...]
    pos_row = pos_ref[...]
    base = pos_ref[0, 0] - j * BLOCK

    def step(t, carry):
        rows = pl.ds(pl.multiple_of(t * BLOCK, BLOCK), BLOCK)
        kt = kv_ref[rows, 0:HEAD_DIM]
        vt = kv_ref[rows, HEAD_DIM : 2 * HEAD_DIM]
        key_pos = base + t * BLOCK + lax.broadcasted_iota(jnp.int32, (BLOCK, BLOCK), 0)
        allowed = (key_pos >= start_row) & (key_pos <= pos_row)
        dq_t, dk, dv = tile_grads(kt, vt, qs_ref, dos_ref, lse_ref, delta_ref, allowed, heads)
        dq_ref[...] += dq_t
        dkv_ref[rows, 0:HEAD_DIM] += dk
        dkv_ref[rows, HEAD_DIM : 2 * HEAD_DIM] += dv
        return carry

    lax.fori_loop(0, j + 1, step, 0)


def rest_kernel(heads, tokens, info, starts_ref, kv3_ref, kv2_ref, kv1_ref, q_ref, do_ref, lse_ref, delta_ref,
                dqa_ref, dkva_ref, first_ref, last_ref, send_ref, keep_ref,
                qs_ref, dos_ref, dq_ref, kv_ref, dkv_ref):
    i = pl.program_id(0)
    window = BACK * tokens
    tiles = window // BLOCK

    @pl.when(i == 0)
    def _():
        for n, ref in enumerate((kv3_ref, kv2_ref, kv1_ref)):
            kv_ref[pl.ds(n * tokens, tokens), :] = ref[...]
        dkv_ref[...] = jnp.zeros_like(dkv_ref)

    base = info[0] * tokens - window
    first = jnp.clip(lax.div(info[5 + i] - base, BLOCK), 0, tiles)
    dq_ref[...] = dqa_ref[...]

    @pl.when(first < tiles)
    def _():
        stack_heads(q_ref, qs_ref, heads)
        stack_heads(do_ref, dos_ref, heads)
        start_row = starts_ref[...]

        def step(t, carry):
            rows = pl.ds(pl.multiple_of(t * BLOCK, BLOCK), BLOCK)
            kt = kv_ref[rows, 0:HEAD_DIM]
            vt = kv_ref[rows, HEAD_DIM : 2 * HEAD_DIM]
            key_pos = base + t * BLOCK + lax.broadcasted_iota(jnp.int32, (BLOCK, BLOCK), 0)
            allowed = key_pos >= start_row
            dq_t, dk, dv = tile_grads(kt, vt, qs_ref, dos_ref, lse_ref, delta_ref, allowed, heads)
            dq_ref[...] += dq_t
            dkv_ref[rows, 0:HEAD_DIM] += dk
            dkv_ref[rows, HEAD_DIM : 2 * HEAD_DIM] += dv
            return carry

        lax.fori_loop(first, tiles, step, 0)

    def put(ref, row):
        for h in range(heads):
            cols = pl.ds(h * HEAD_DIM, HEAD_DIM)
            ref[pl.ds(row, BLOCK), cols] = (dq_ref[:, cols].T * SCALE).astype(jnp.bfloat16)

    @pl.when(i < 2)
    def _():
        put(first_ref, pl.multiple_of(i * BLOCK, BLOCK))

    @pl.when(i == 2)
    def _():
        put(last_ref, 0)
        side = info[1]
        half = HEAD_DIM // 2
        left = lax.broadcasted_iota(jnp.int32, (tokens, HEAD_DIM), 1) < half
        for n in range(BACK + 1):
            rows = pl.ds(n * tokens, tokens)
            if n < BACK:
                dk, dv = dkv_ref[rows, 0:HEAD_DIM], dkv_ref[rows, HEAD_DIM : 2 * HEAD_DIM]
            else:
                dk, dv = dkva_ref[:, 0:HEAD_DIM], dkva_ref[:, HEAD_DIM : 2 * HEAD_DIM]
            dk = dk * SCALE
            low = jnp.where(left, dk, pltpu.roll(dv, half, 1))
            high = jnp.where(left, pltpu.roll(dk, half, 1), dv)
            keep_ref[rows, :] = jnp.where(side == 0, low, high)
            send_ref[rows, :] = jnp.where(side == 0, high, low).astype(jnp.bfloat16)


def place_kernel(info, mine12, mine3, theirs12, theirs3, out, sems):
    for s in range(3):
        source = info[8 + s]
        dst = out.at[pl.ds(s * BLOCK, BLOCK), :]

        def copy(src, s=s, dst=dst):
            return pltpu.make_async_copy(src, dst, sems.at[s])

        for number, array in enumerate((mine12, theirs12)):
            @pl.when((source == 3 * number) | (source == 3 * number + 1))
            def _(array=array, number=number, source=source, copy=copy):
                row = pl.multiple_of(jnp.clip(source - 3 * number, 0, 1) * BLOCK, BLOCK)
                copy(array.at[pl.ds(row, BLOCK), :]).start()
        for number, array in enumerate((mine3, theirs3)):
            @pl.when(source == 3 * number + 2)
            def _(array=array, copy=copy):
                copy(array).start()
    for s in range(3):
        pltpu.make_async_copy(mine3, out.at[pl.ds(s * BLOCK, BLOCK), :], sems.at[s]).wait()


def plan_info(block_plan, starts, seq_index, head_index, per_device, half_axis):
    partner = seq_index ^ half_axis
    mine = lax.dynamic_slice_in_dim(block_plan, seq_index * per_device, per_device)
    theirs = lax.dynamic_slice_in_dim(block_plan, partner * per_device, per_device)
    wanted = theirs // per_device == seq_index
    local = jnp.arange(per_device, dtype=jnp.int32)
    is_it = (theirs[None, :] == (seq_index * per_device + local)[:, None]) & wanted[None, :]
    sent = jnp.any(is_it, axis=1)
    slot = jnp.sum(jnp.where(is_it, local[None, :], 0), axis=1)
    rank_key = jnp.where(sent, slot, per_device + local)
    position = jnp.sum((rank_key[None, :] < rank_key[:, None]).astype(jnp.int32), axis=1)
    order = jnp.sum(jnp.where(position[None, :] == local[:, None], local[None, :], 0), axis=1)
    block_starts = starts.reshape(per_device, BLOCK)[:, 0]
    order_starts = jnp.sum(jnp.where(order[:, None] == local[None, :], block_starts[None, :], 0), axis=1)
    far = mine // per_device != seq_index
    far_rank = jnp.cumsum(far.astype(jnp.int32)) - 1
    near_pos = jnp.sum(jnp.where((mine % per_device)[:, None] == local[None, :], position[None, :], 0), axis=1)
    source = jnp.where(far, per_device + far_rank, near_pos)
    head = jnp.stack([seq_index, head_index % 2])
    return jnp.concatenate([head, order, order_starts, source]).astype(jnp.int32)


def on_device(queries, key_states, value_states, attn_out, grad_out, log_norm, lengths, block_plan):
    tokens = queries.shape[0]
    feature = queries.shape[1]
    heads = feature // HEAD_DIM
    per_device = tokens // BLOCK
    seq_index = lax.axis_index("seq")
    head_index = lax.axis_index("head")
    half_axis = lax.axis_size("seq") // 2
    kv_group = head_index // 2
    own_kv = jnp.concatenate([
        lax.dynamic_slice_in_dim(key_states, kv_group * HEAD_DIM, HEAD_DIM, 1),
        lax.dynamic_slice_in_dim(value_states, kv_group * HEAD_DIM, HEAD_DIM, 1)], axis=1)
    kv3, kv2, kv1 = (shifted(own_kv, "seq", n) for n in (3, 2, 1))

    doc_ends = jnp.cumsum(lengths)
    doc_begins = doc_ends - lengths
    pos = seq_index * tokens + jnp.arange(tokens, dtype=jnp.int32)
    starts = jnp.max(jnp.where(doc_begins[:, None] <= pos[None, :], doc_begins[:, None], 0), axis=0)
    info = plan_info(block_plan, starts, seq_index, head_index, per_device, half_axis)
    starts = starts.reshape(1, tokens)
    pos = pos.reshape(1, tokens)

    f32, bf16 = jnp.float32, jnp.bfloat16
    row_block = pl.BlockSpec((BLOCK, feature), lambda j: (j, 0))
    lane_row = pl.BlockSpec((1, BLOCK), lambda j: (0, j))
    own_dq, own_dkv, delta = pl.pallas_call(
        functools.partial(own_kernel, heads),
        grid=(per_device,),
        in_specs=[lane_row, lane_row,
                  pl.BlockSpec((tokens, 2 * HEAD_DIM), lambda j: (0, 0)),
                  row_block, row_block, row_block,
                  pl.BlockSpec((heads, BLOCK), lambda j: (0, j))],
        out_specs=[row_block,
                   pl.BlockSpec((tokens, 2 * HEAD_DIM), lambda j: (0, 0)),
                   pl.BlockSpec((heads, BLOCK), lambda j: (0, j))],
        out_shape=[jax.ShapeDtypeStruct((tokens, feature), f32),
                   jax.ShapeDtypeStruct((tokens, 2 * HEAD_DIM), f32),
                   jax.ShapeDtypeStruct((heads, tokens), f32)],
        scratch_shapes=[pltpu.VMEM((feature, HEAD_DIM), bf16), pltpu.VMEM((feature, HEAD_DIM), bf16)],
        compiler_params=pltpu.CompilerParams(vmem_limit_bytes=32 * 2**20),
        cost_estimate=pl.CostEstimate(flops=2_000_000_000, bytes_accessed=4_000_000, transcendentals=600_000),
        name="own_keys",
    )(starts, pos, own_kv, queries, attn_out, grad_out, log_norm)

    picked = lambda i, info: (info[2 + i], 0)
    picked_lane = lambda i, info: (0, info[2 + i])
    fixed = lambda i, info: (0, 0)
    picked_rows = pl.BlockSpec((BLOCK, feature), picked)
    kv_spec = pl.BlockSpec((tokens, 2 * HEAD_DIM), fixed)
    window = BACK * tokens
    dq12, dq3, send, keep = pl.pallas_call(
        functools.partial(rest_kernel, heads, tokens),
        grid_spec=pltpu.PrefetchScalarGridSpec(
            num_scalar_prefetch=1,
            grid=(per_device,),
            in_specs=[pl.BlockSpec((1, BLOCK), picked_lane), kv_spec, kv_spec, kv_spec,
                      picked_rows, picked_rows,
                      pl.BlockSpec((heads, BLOCK), picked_lane), pl.BlockSpec((heads, BLOCK), picked_lane),
                      picked_rows, kv_spec],
            out_specs=[pl.BlockSpec((2 * BLOCK, feature), fixed), pl.BlockSpec((BLOCK, feature), fixed),
                       pl.BlockSpec((window + tokens, HEAD_DIM), fixed),
                       pl.BlockSpec((window + tokens, HEAD_DIM), fixed)],
            scratch_shapes=[pltpu.VMEM((feature, HEAD_DIM), bf16), pltpu.VMEM((feature, HEAD_DIM), bf16),
                            pltpu.VMEM((BLOCK, feature), f32),
                            pltpu.VMEM((window, 2 * HEAD_DIM), bf16), pltpu.VMEM((window, 2 * HEAD_DIM), f32)]),
        out_shape=[jax.ShapeDtypeStruct((2 * BLOCK, feature), bf16),
                   jax.ShapeDtypeStruct((BLOCK, feature), bf16),
                   jax.ShapeDtypeStruct((window + tokens, HEAD_DIM), bf16),
                   jax.ShapeDtypeStruct((window + tokens, HEAD_DIM), f32)],
        compiler_params=pltpu.CompilerParams(vmem_limit_bytes=32 * 2**20),
        cost_estimate=pl.CostEstimate(flops=2_000_000_000, bytes_accessed=4_000_000, transcendentals=600_000),
        name="rest_keys",
    )(info, starts, kv3, kv2, kv1, queries, grad_out, log_norm, delta, own_dq, own_dkv)

    far12 = swapped(dq12, "seq", half_axis)
    far3 = swapped(dq3, "seq", half_axis)

    arrived = swapped(send, "head", 1)
    both = keep + arrived.astype(f32)
    total = both[window:]
    for n in (3, 2, 1):
        piece = both[(BACK - n) * tokens : (BACK - n + 1) * tokens].astype(bf16)
        total = total + shifted(piece, "seq", -n).astype(f32)
    total = total.astype(bf16)
    half = HEAD_DIM // 2

    anywhere = pl.BlockSpec(memory_space=pl.ANY)
    query_grad = pl.pallas_call(
        place_kernel,
        in_specs=[pl.BlockSpec(memory_space=pltpu.SMEM)] + [anywhere] * 4,
        out_specs=anywhere,
        out_shape=jax.ShapeDtypeStruct((tokens, feature), bf16),
        scratch_shapes=[pltpu.SemaphoreType.DMA((3,))],
        name="place_blocks",
    )(info, dq12, dq3, far12, far3)
    return query_grad, total[:, :half], total[:, half:]


def solution(mesh):
    placed = (
        P("seq", "head"),
        P("seq", None),
        P("seq", None),
        P("seq", "head"),
        P("seq", "head"),
        P("head", "seq"),
        P(),
        P(),
    )
    return jax.shard_map(
        on_device,
        mesh=mesh,
        in_specs=placed,
        out_specs=(P("seq", "head"), P("seq", "head"), P("seq", "head")),
        check_vma=False,
    )
```

```python
import functools

import jax
import jax.numpy as jnp
from jax import lax
from jax.experimental import pallas as pl
from jax.experimental.pallas import tpu as pltpu
from jax.sharding import PartitionSpec as P

HEAD_DIM = 128
BLOCK = 128
BACK = 3
VMEM_LIMIT = 56 * 2**20
LOG2E = 1.4426950408889634
SCALE = HEAD_DIM ** -0.5


def shifted(value, axis, steps):
    count = lax.axis_size(axis)
    first, last = (max(0, -steps), min(count, count - steps))
    return lax.ppermute(value, axis, [(i, i + steps) for i in range(first, last)])


def swapped(array, axis, apart):
    return lax.ppermute(array, axis, [(i, i ^ apart) for i in range(lax.axis_size(axis))])


def dot(a, b):
    return jnp.dot(a, b, preferred_element_type=jnp.float32)


def dot_nt(a, b):
    return lax.dot_general(a, b, (((1,), (1,)), ((), ())), preferred_element_type=jnp.float32)


def stack_heads(wide_ref, stacked_ref, heads):
    for h in range(heads):
        stacked_ref[pl.ds(h * HEAD_DIM, HEAD_DIM), :] = wide_ref[:, pl.ds(h * HEAD_DIM, HEAD_DIM)]


def tile_grads(kt, vt, qs_ref, dos_ref, lse_ref, delta_ref, allowed, heads):
    scores = dot_nt(kt, qs_ref[...])
    prob_grad = dot_nt(vt, dos_ref[...])
    weights, score_grads = [], []
    for h in range(heads):
        cols = slice(h * BLOCK, (h + 1) * BLOCK)
        lse = lse_ref[h : h + 1, :].astype(jnp.float32) * LOG2E
        w = jnp.where(allowed, jnp.exp2(scores[:, cols] * (SCALE * LOG2E) - lse), 0.0)
        weights.append(w.astype(jnp.bfloat16))
        score_grads.append((w * (prob_grad[:, cols] - delta_ref[h : h + 1, :])).astype(jnp.bfloat16))
    w_half = jnp.concatenate(weights, axis=1)
    s_grad = jnp.concatenate(score_grads, axis=1)
    dv = dot(w_half, dos_ref[...])
    dk = dot(s_grad, qs_ref[...])
    dq_t = dot(kt.T, s_grad)
    return dq_t, dk, dv


def plan_info(info_ref, lengths_ref, plan_ref, device, partner, side, per_device):
    first = device * per_device
    locals_ = range(per_device)
    theirs = [plan_ref[partner * per_device + s] for s in locals_]
    mine = [plan_ref[first + s] for s in locals_]
    ranks = []
    for l in locals_:
        rank = per_device + l
        for s in locals_:
            rank = jnp.where(theirs[s] == first + l, s, rank)
        ranks.append(rank)
    position = [sum((ranks[m] < ranks[l]).astype(jnp.int32) for m in locals_ if m != l) for l in locals_]
    starts = [jnp.int32(0)] * per_device
    begin = jnp.int32(0)
    for n in range(lengths_ref.shape[0]):
        starts = [jnp.where(begin <= (first + l) * BLOCK, begin, starts[l]) for l in locals_]
        begin = begin + lengths_ref[n]
    info_ref[0] = device
    info_ref[1] = side
    for i in locals_:
        info_ref[2 + i] = sum(jnp.where(position[l] == i, l, 0) for l in locals_)
        info_ref[5 + i] = sum(jnp.where(position[l] == i, starts[l], 0) for l in locals_)
    far_rank = jnp.int32(0)
    for s in locals_:
        local = mine[s] - first
        near = (local >= 0) & (local < per_device)
        near_position = sum(jnp.where(local == l, position[l], 0) for l in locals_)
        info_ref[8 + s] = jnp.where(near, near_position, per_device + far_rank)
        far_rank = far_rank + jnp.where(near, 0, 1)


def own_kernel(heads, half_axis, lengths_ref, plan_ref, kv_ref, q_ref, o_ref, do_ref, lse_ref,
               dq_ref, dkv_ref, delta_ref, starts_ref, info_ref, qs_ref, dos_ref):
    j = pl.program_id(0)
    per_device = pl.num_programs(0)
    device = lax.axis_index("seq")
    base = device * kv_ref.shape[0]

    @pl.when(j == 0)
    def _():
        dkv_ref[...] = jnp.zeros_like(dkv_ref)
        plan_info(info_ref, lengths_ref, plan_ref, device, device ^ half_axis,
                  lax.axis_index("head") & 1, kv_ref.shape[0] // BLOCK)

    stack_heads(q_ref, qs_ref, heads)
    stack_heads(do_ref, dos_ref, heads)
    ones = jnp.ones((8, 2 * HEAD_DIM), jnp.bfloat16)
    for h in range(heads):
        cols = pl.ds(h * HEAD_DIM, HEAD_DIM)
        prod = do_ref[:, cols].astype(jnp.float32) * o_ref[:, cols].astype(jnp.float32)
        high = prod.astype(jnp.bfloat16)
        low = (prod - high.astype(jnp.float32)).astype(jnp.bfloat16)
        row = dot_nt(ones, jnp.concatenate([high, low], axis=1))
        delta_ref[h : h + 1, :] = row[0:1, :]
    dq_ref[...] = jnp.zeros_like(dq_ref)
    pos_row = base + j * BLOCK + lax.broadcasted_iota(jnp.int32, (1, BLOCK), 1)
    start_row = jnp.zeros((1, BLOCK), jnp.int32)
    begin = jnp.int32(0)
    for n in range(lengths_ref.shape[0]):
        start_row = jnp.where(pos_row >= begin, begin, start_row)
        begin = begin + lengths_ref[n]
    starts_ref[...] = start_row

    def step(t, carry):
        rows = pl.ds(pl.multiple_of(t * BLOCK, BLOCK), BLOCK)
        kt = kv_ref[rows, 0:HEAD_DIM]
        vt = kv_ref[rows, HEAD_DIM : 2 * HEAD_DIM]
        key_pos = base + t * BLOCK + lax.broadcasted_iota(jnp.int32, (BLOCK, BLOCK), 0)
        allowed = (key_pos >= start_row) & (key_pos <= pos_row)
        dq_t, dk, dv = tile_grads(kt, vt, qs_ref, dos_ref, lse_ref, delta_ref, allowed, heads)
        dq_ref[...] += dq_t
        dkv_ref[rows, 0:HEAD_DIM] += dk
        dkv_ref[rows, HEAD_DIM : 2 * HEAD_DIM] += dv
        return carry

    lax.fori_loop(0, j + 1, step, 0)


def rest_kernel(heads, tokens, info, starts_ref, kv3_ref, kv2_ref, kv1_ref, q_ref, do_ref, lse_ref, delta_ref,
                dqa_ref, dkva_ref, first_ref, last_ref, send_ref, keep_ref,
                qs_ref, dos_ref, dq_ref, kv_ref, dkv_ref):
    i = pl.program_id(0)
    window = BACK * tokens
    tiles = window // BLOCK

    @pl.when(i == 0)
    def _():
        for n, ref in enumerate((kv3_ref, kv2_ref, kv1_ref)):
            kv_ref[pl.ds(n * tokens, tokens), :] = ref[...]
        dkv_ref[...] = jnp.zeros_like(dkv_ref)

    base = info[0] * tokens - window
    first = jnp.clip(lax.div(info[5 + i] - base, BLOCK), 0, tiles)
    dq_ref[...] = dqa_ref[...]

    @pl.when(first < tiles)
    def _():
        stack_heads(q_ref, qs_ref, heads)
        stack_heads(do_ref, dos_ref, heads)
        start_row = starts_ref[...]

        def step(t, carry):
            rows = pl.ds(pl.multiple_of(t * BLOCK, BLOCK), BLOCK)
            kt = kv_ref[rows, 0:HEAD_DIM]
            vt = kv_ref[rows, HEAD_DIM : 2 * HEAD_DIM]
            key_pos = base + t * BLOCK + lax.broadcasted_iota(jnp.int32, (BLOCK, BLOCK), 0)
            allowed = key_pos >= start_row
            dq_t, dk, dv = tile_grads(kt, vt, qs_ref, dos_ref, lse_ref, delta_ref, allowed, heads)
            dq_ref[...] += dq_t
            dkv_ref[rows, 0:HEAD_DIM] += dk
            dkv_ref[rows, HEAD_DIM : 2 * HEAD_DIM] += dv
            return carry

        lax.fori_loop(first, tiles, step, 0)

    def put(ref, row):
        for h in range(heads):
            cols = pl.ds(h * HEAD_DIM, HEAD_DIM)
            ref[pl.ds(row, BLOCK), cols] = (dq_ref[:, cols].T * SCALE).astype(jnp.bfloat16)

    @pl.when(i < 2)
    def _():
        put(first_ref, pl.multiple_of(i * BLOCK, BLOCK))

    @pl.when(i == 2)
    def _():
        put(last_ref, 0)
        side = info[1]
        half = HEAD_DIM // 2
        left = lax.broadcasted_iota(jnp.int32, (tokens, HEAD_DIM), 1) < half
        for n in range(BACK + 1):
            rows = pl.ds(n * tokens, tokens)
            if n < BACK:
                dk, dv = dkv_ref[rows, 0:HEAD_DIM], dkv_ref[rows, HEAD_DIM : 2 * HEAD_DIM]
            else:
                dk, dv = dkva_ref[:, 0:HEAD_DIM], dkva_ref[:, HEAD_DIM : 2 * HEAD_DIM]
            dk = dk * SCALE
            low = jnp.where(left, dk, pltpu.roll(dv, half, 1))
            high = jnp.where(left, pltpu.roll(dk, half, 1), dv)
            keep_ref[rows, :] = jnp.where(side == 0, low, high)
            send_ref[rows, :] = jnp.where(side == 0, high, low).astype(jnp.bfloat16)


def finish_kernel(info, mine12, mine3, theirs12, theirs3, own_ref, r1_ref, r2_ref, r3_ref,
                  out_ref, key_ref, value_ref, sems):
    for s in range(3):
        source = info[8 + s]
        dst = out_ref.at[pl.ds(s * BLOCK, BLOCK), :]

        def copy(src, s=s, dst=dst):
            return pltpu.make_async_copy(src, dst, sems.at[s])

        for number, array in enumerate((mine12, theirs12)):
            @pl.when((source == 3 * number) | (source == 3 * number + 1))
            def _(array=array, number=number, source=source, copy=copy):
                row = pl.multiple_of(jnp.clip(source - 3 * number, 0, 1) * BLOCK, BLOCK)
                copy(array.at[pl.ds(row, BLOCK), :]).start()
        for number, array in enumerate((mine3, theirs3)):
            @pl.when(source == 3 * number + 2)
            def _(array=array, copy=copy):
                copy(array).start()
    total = own_ref[...]
    for ref in (r1_ref, r2_ref, r3_ref):
        total = total + ref[...].astype(jnp.float32)
    half = HEAD_DIM // 2
    key_ref[...] = total[:, :half].astype(jnp.bfloat16)
    value_ref[...] = total[:, half:].astype(jnp.bfloat16)
    for s in range(3):
        pltpu.make_async_copy(mine3, out_ref.at[pl.ds(s * BLOCK, BLOCK), :], sems.at[s]).wait()


GROUPS = 4


def third_needed(block_plan, per_device, half_axis):
    holder = block_plan.reshape(-1, per_device)[:half_axis] // per_device
    here = jnp.arange(half_axis, dtype=jnp.int32)
    full = jnp.all(holder != here[:, None], axis=1)
    return sum(jnp.max(jnp.where(full & (here % GROUPS == g), 1 << g, 0)) for g in range(GROUPS))


def on_device(queries, key_states, value_states, attn_out, grad_out, log_norm, lengths, block_plan):
    tokens = queries.shape[0]
    feature = queries.shape[1]
    heads = feature // HEAD_DIM
    per_device = tokens // BLOCK
    half_axis = lax.axis_size("seq") // 2
    window = BACK * tokens
    kv_group = lax.axis_index("head") // 2
    own_kv = jnp.concatenate([
        lax.dynamic_slice_in_dim(key_states, kv_group * HEAD_DIM, HEAD_DIM, 1),
        lax.dynamic_slice_in_dim(value_states, kv_group * HEAD_DIM, HEAD_DIM, 1)], axis=1)
    kv3, kv2, kv1 = (shifted(own_kv, "seq", n) for n in (3, 2, 1))
    branch = third_needed(block_plan, per_device, half_axis)

    f32, bf16 = jnp.float32, jnp.bfloat16
    smem = pl.BlockSpec(memory_space=pltpu.SMEM)
    row_block = pl.BlockSpec((BLOCK, feature), lambda j: (j, 0))
    own_dq, own_dkv, delta, starts, info = pl.pallas_call(
        functools.partial(own_kernel, heads, half_axis),
        grid=(per_device,),
        in_specs=[smem, smem,
                  pl.BlockSpec((tokens, 2 * HEAD_DIM), lambda j: (0, 0)),
                  row_block, row_block, row_block,
                  pl.BlockSpec((heads, BLOCK), lambda j: (0, j))],
        out_specs=[row_block,
                   pl.BlockSpec((tokens, 2 * HEAD_DIM), lambda j: (0, 0)),
                   pl.BlockSpec((heads, BLOCK), lambda j: (0, j)),
                   pl.BlockSpec((1, BLOCK), lambda j: (0, j)),
                   smem],
        out_shape=[jax.ShapeDtypeStruct((tokens, feature), f32),
                   jax.ShapeDtypeStruct((tokens, 2 * HEAD_DIM), f32),
                   jax.ShapeDtypeStruct((heads, tokens), f32),
                   jax.ShapeDtypeStruct((1, tokens), jnp.int32),
                   jax.ShapeDtypeStruct((16,), jnp.int32)],
        scratch_shapes=[pltpu.VMEM((feature, HEAD_DIM), bf16), pltpu.VMEM((feature, HEAD_DIM), bf16)],
        compiler_params=pltpu.CompilerParams(vmem_limit_bytes=VMEM_LIMIT),
        cost_estimate=pl.CostEstimate(flops=2_000_000_000, bytes_accessed=4_000_000, transcendentals=600_000),
        name="own_keys",
    )(lengths, block_plan, own_kv, queries, attn_out, grad_out, log_norm)

    picked = lambda i, info: (info[2 + i], 0)
    picked_lane = lambda i, info: (0, info[2 + i])
    fixed = lambda i, info: (0, 0)
    picked_rows = pl.BlockSpec((BLOCK, feature), picked)
    kv_spec = pl.BlockSpec((tokens, 2 * HEAD_DIM), fixed)
    dq12, dq3, send, keep = pl.pallas_call(
        functools.partial(rest_kernel, heads, tokens),
        grid_spec=pltpu.PrefetchScalarGridSpec(
            num_scalar_prefetch=1,
            grid=(per_device,),
            in_specs=[pl.BlockSpec((1, BLOCK), picked_lane), kv_spec, kv_spec, kv_spec,
                      picked_rows, picked_rows,
                      pl.BlockSpec((heads, BLOCK), picked_lane), pl.BlockSpec((heads, BLOCK), picked_lane),
                      picked_rows, kv_spec],
            out_specs=[pl.BlockSpec((2 * BLOCK, feature), fixed), pl.BlockSpec((BLOCK, feature), fixed),
                       pl.BlockSpec((window + tokens, HEAD_DIM), fixed),
                       pl.BlockSpec((window + tokens, HEAD_DIM), fixed)],
            scratch_shapes=[pltpu.VMEM((feature, HEAD_DIM), bf16), pltpu.VMEM((feature, HEAD_DIM), bf16),
                            pltpu.VMEM((BLOCK, feature), f32),
                            pltpu.VMEM((window, 2 * HEAD_DIM), bf16), pltpu.VMEM((window, 2 * HEAD_DIM), f32)]),
        out_shape=[jax.ShapeDtypeStruct((2 * BLOCK, feature), bf16),
                   jax.ShapeDtypeStruct((BLOCK, feature), bf16),
                   jax.ShapeDtypeStruct((window + tokens, HEAD_DIM), bf16),
                   jax.ShapeDtypeStruct((window + tokens, HEAD_DIM), f32)],
        compiler_params=pltpu.CompilerParams(vmem_limit_bytes=VMEM_LIMIT),
        cost_estimate=pl.CostEstimate(flops=2_000_000_000, bytes_accessed=4_000_000, transcendentals=600_000),
        name="rest_keys",
    )(info, starts, kv3, kv2, kv1, queries, grad_out, log_norm, delta, own_dq, own_dkv)

    far12 = swapped(dq12, "seq", half_axis)

    def returns(mask, dq3, send, keep):
        pairs = [(i, i ^ half_axis) for i in range(2 * half_axis) if mask >> (i % half_axis % GROUPS) & 1]
        far3 = lax.ppermute(dq3, "seq", pairs) if pairs else dq3
        both = keep + swapped(send, "head", 1).astype(f32)
        pieces = [both[(BACK - n) * tokens : (BACK - n + 1) * tokens].astype(bf16) for n in (3, 2, 1)]
        back = [shifted(piece, "seq", -n) for piece, n in zip(pieces, (3, 2, 1))]
        return (far3, both[window:], *back)

    branches = [functools.partial(returns, mask) for mask in range(1 << GROUPS)]
    far3, own, back3, back2, back1 = lax.switch(branch, branches, dq3, send, keep)

    anywhere = pl.BlockSpec(memory_space=pl.ANY)
    vmem = pl.BlockSpec(memory_space=pltpu.VMEM)
    grad_half = jax.ShapeDtypeStruct((tokens, HEAD_DIM // 2), bf16)
    return pl.pallas_call(
        finish_kernel,
        in_specs=[smem] + [anywhere] * 4 + [vmem] * 4,
        out_specs=[vmem] * 3,
        out_shape=[jax.ShapeDtypeStruct((tokens, feature), bf16), grad_half, grad_half],
        scratch_shapes=[pltpu.SemaphoreType.DMA((3,))],
        name="place_blocks",
    )(info, dq12, dq3, far12, far3, own, back1, back2, back3)


def solution(mesh):
    placed = (
        P("seq", "head"),
        P("seq", None),
        P("seq", None),
        P("seq", "head"),
        P("seq", "head"),
        P("head", "seq"),
        P(),
        P(),
    )
    return jax.shard_map(
        on_device,
        mesh=mesh,
        in_specs=placed,
        out_specs=(P("seq", "head"), P("seq", "head"), P("seq", "head")),
        check_vma=False,
    )
```

```python
import functools

import jax
import jax.numpy as jnp
from jax import lax
from jax.experimental import pallas as pl
from jax.experimental.pallas import tpu as pltpu
from jax.sharding import PartitionSpec as P

HEAD_DIM = 128
BLOCK = 128
BACK = 3
VMEM_LIMIT = 20 * 2**20
GROUPS = 4
LOG2E = 1.4426950408889634
SCALE = HEAD_DIM ** -0.5


def shifted(value, axis, steps):
    count = lax.axis_size(axis)
    first, last = (max(0, -steps), min(count, count - steps))
    return lax.ppermute(value, axis, [(i, i + steps) for i in range(first, last)])


def swapped(array, axis, apart):
    return lax.ppermute(array, axis, [(i, i ^ apart) for i in range(lax.axis_size(axis))])


def dot(a, b):
    return jnp.dot(a, b, preferred_element_type=jnp.float32)


def dot_nt(a, b):
    return lax.dot_general(a, b, (((1,), (1,)), ((), ())), preferred_element_type=jnp.float32)


def tile_grads(kt, vt, qs, dos, rows, allowed, heads):
    scores = dot_nt(kt, qs)
    prob_grad = dot_nt(vt, dos)
    weights, score_grads = [], []
    for h in range(heads):
        cols = slice(h * BLOCK, (h + 1) * BLOCK)
        lse = rows[h : h + 1, :]
        delta = rows[heads + h : heads + h + 1, :]
        w = jnp.where(allowed, jnp.exp2(scores[:, cols] * (SCALE * LOG2E) - lse), 0.0)
        weights.append(w.astype(jnp.bfloat16))
        score_grads.append((w * (prob_grad[:, cols] - delta)).astype(jnp.bfloat16))
    w_half = jnp.concatenate(weights, axis=1)
    s_grad = jnp.concatenate(score_grads, axis=1)
    dv = dot(w_half, dos)
    dk = dot(s_grad, qs)
    dq_t = dot(kt.T, s_grad)
    return dq_t, dk, dv


def plan_info(info_ref, branch_ref, lengths_ref, plan_ref, device, half_axis, side, per_device):
    first = device * per_device
    partner = device ^ half_axis
    locals_ = range(per_device)
    theirs = [plan_ref[partner * per_device + s] for s in locals_]
    mine = [plan_ref[first + s] for s in locals_]
    ranks = []
    for l in locals_:
        rank = per_device + l
        for s in locals_:
            rank = jnp.where(theirs[s] == first + l, s, rank)
        ranks.append(rank)
    position = [sum((ranks[m] < ranks[l]).astype(jnp.int32) for m in locals_ if m != l) for l in locals_]
    starts = [jnp.int32(0)] * per_device
    begin = jnp.int32(0)
    for n in range(lengths_ref.shape[0]):
        starts = [jnp.where(begin <= (first + l) * BLOCK, begin, starts[l]) for l in locals_]
        begin = begin + lengths_ref[n]
    info_ref[0] = device
    info_ref[1] = side
    for i in locals_:
        info_ref[2 + i] = sum(jnp.where(position[l] == i, l, 0) for l in locals_)
        info_ref[5 + i] = sum(jnp.where(position[l] == i, starts[l], 0) for l in locals_)
    far_rank = jnp.int32(0)
    for s in locals_:
        local = mine[s] - first
        near = (local >= 0) & (local < per_device)
        near_position = sum(jnp.where(local == l, position[l], 0) for l in locals_)
        info_ref[8 + s] = jnp.where(near, near_position, per_device + far_rank)
        far_rank = far_rank + jnp.where(near, 0, 1)
    mask = jnp.int32(0)
    for pair in range(half_axis):
        full = jnp.bool_(True)
        for s in locals_:
            local = plan_ref[pair * per_device + s] - pair * per_device
            full = full & ((local < 0) | (local >= per_device))
        mask = mask | jnp.where(full, 1 << (pair % GROUPS), 0)
    branch_ref[0] = mask


def own_kernel(heads, half_axis, lengths_ref, plan_ref, kv_ref, q_hbm, o_hbm, do_hbm, lse_ref,
               dq_ref, dkv_ref, rows_ref, starts_ref, qs_ref, dos_ref, info_ref, branch_ref,
               q_buf, o_buf, do_buf, sems):
    tokens = kv_ref.shape[0]
    blocks = tokens // BLOCK
    feature = heads * HEAD_DIM

    def copies(j):
        rows = pl.ds(j * BLOCK, BLOCK)
        pairs = ((do_hbm, do_buf), (o_hbm, o_buf), (q_hbm, q_buf))
        return [pltpu.make_async_copy(a.at[rows, :], b.at[rows, :], sems.at[j, n]) for n, (a, b) in enumerate(pairs)]

    for j in range(blocks):
        for c in copies(j):
            c.start()
    device = lax.axis_index("seq")
    base = device * tokens
    dkv_ref[...] = jnp.zeros_like(dkv_ref)
    plan_info(info_ref, branch_ref, lengths_ref, plan_ref, device, half_axis, lax.axis_index("head") & 1, blocks)

    pos = base + lax.broadcasted_iota(jnp.int32, (1, tokens), 1)
    start = jnp.zeros((1, tokens), jnp.int32)
    begin = jnp.int32(0)
    for n in range(lengths_ref.shape[0]):
        start = jnp.where(pos >= begin, begin, start)
        begin = begin + lengths_ref[n]

    ones = jnp.ones((8, 2 * HEAD_DIM), jnp.bfloat16)
    for j in range(blocks):
        rows = pl.ds(j * BLOCK, BLOCK)
        lanes = slice(j * BLOCK, (j + 1) * BLOCK)
        for c in copies(j):
            c.wait()
        for h in range(heads):
            cols = pl.ds(h * HEAD_DIM, HEAD_DIM)
            stacked = pl.ds(j * feature + h * HEAD_DIM, HEAD_DIM)
            qs_ref[stacked, :] = q_buf[rows, cols]
            dos_ref[stacked, :] = do_buf[rows, cols]
            prod = do_buf[rows, cols].astype(jnp.float32) * o_buf[rows, cols].astype(jnp.float32)
            high = prod.astype(jnp.bfloat16)
            low = (prod - high.astype(jnp.float32)).astype(jnp.bfloat16)
            row = dot_nt(ones, jnp.concatenate([high, low], axis=1))
            rows_ref[j, heads + h : heads + h + 1, :] = row[0:1, :]
        rows_ref[j, 0:heads, :] = lse_ref[:, lanes].astype(jnp.float32) * LOG2E
        start_row, pos_row = start[:, lanes], pos[:, lanes]
        starts_ref[j] = jnp.broadcast_to(start_row, (8, BLOCK))
        dq_ref[rows, :] = jnp.zeros((BLOCK, feature), jnp.float32)

        def step(t, carry, j=j, rows=rows, start_row=start_row, pos_row=pos_row):
            keys = pl.ds(pl.multiple_of(t * BLOCK, BLOCK), BLOCK)
            queries = pl.ds(j * feature, feature)
            key_pos = base + t * BLOCK + lax.broadcasted_iota(jnp.int32, (BLOCK, BLOCK), 0)
            allowed = (key_pos >= start_row) & (key_pos <= pos_row)
            dq_t, dk, dv = tile_grads(kv_ref[keys, 0:HEAD_DIM], kv_ref[keys, HEAD_DIM : 2 * HEAD_DIM],
                                      qs_ref[queries, :], dos_ref[queries, :], rows_ref.at[j], allowed, heads)
            dq_ref[rows, :] += dq_t
            dkv_ref[keys, 0:HEAD_DIM] += dk
            dkv_ref[keys, HEAD_DIM : 2 * HEAD_DIM] += dv
            return carry

        lax.fori_loop(0, j + 1, step, 0)


def rest_kernel(heads, info, starts_ref, kv3_ref, kv2_ref, kv1_ref, qs_ref, dos_ref, rows_ref, dqa_ref, dkva_ref,
                first_ref, last_ref, send_ref, far_ref, own_ref, dq_ref, kv_ref, dkv_ref):
    tokens = dkva_ref.shape[0]
    blocks = tokens // BLOCK
    feature = heads * HEAD_DIM
    window = BACK * tokens
    tiles = window // BLOCK
    for n, ref in enumerate((kv3_ref, kv2_ref, kv1_ref)):
        kv_ref[pl.ds(n * tokens, tokens), :] = ref[...]
    dkv_ref[...] = jnp.zeros_like(dkv_ref)
    base = info[0] * tokens - window
    for i in range(blocks):
        block = jnp.clip(info[2 + i], 0, blocks - 1)
        first = jnp.clip(lax.div(info[5 + i] - base, BLOCK), 0, tiles)
        queries = pl.ds(pl.multiple_of(block * feature, feature), feature)
        dq_ref[...] = dqa_ref[pl.ds(pl.multiple_of(block * BLOCK, BLOCK), BLOCK), :]
        start_row = starts_ref[block, 0:1, :]

        def step(t, carry, block=block, queries=queries, start_row=start_row):
            keys = pl.ds(pl.multiple_of(t * BLOCK, BLOCK), BLOCK)
            key_pos = base + t * BLOCK + lax.broadcasted_iota(jnp.int32, (BLOCK, BLOCK), 0)
            dq_t, dk, dv = tile_grads(kv_ref[keys, 0:HEAD_DIM], kv_ref[keys, HEAD_DIM : 2 * HEAD_DIM],
                                      qs_ref[queries, :], dos_ref[queries, :], rows_ref.at[block],
                                      key_pos >= start_row, heads)
            dq_ref[...] += dq_t
            dkv_ref[keys, 0:HEAD_DIM] += dk
            dkv_ref[keys, HEAD_DIM : 2 * HEAD_DIM] += dv
            return carry

        lax.fori_loop(first, tiles, step, 0)
        out, row = (first_ref, i * BLOCK) if i < 2 else (last_ref, 0)
        for h in range(heads):
            cols = pl.ds(h * HEAD_DIM, HEAD_DIM)
            out[pl.ds(row, BLOCK), cols] = (dq_ref[:, cols].T * SCALE).astype(jnp.bfloat16)

    side = info[1]
    half = HEAD_DIM // 2
    left = lax.broadcasted_iota(jnp.int32, (tokens, HEAD_DIM), 1) < half
    for n in range(BACK + 1):
        rows = pl.ds(n * tokens, tokens)
        if n < BACK:
            dk, dv = dkv_ref[rows, 0:HEAD_DIM], dkv_ref[rows, HEAD_DIM : 2 * HEAD_DIM]
        else:
            dk, dv = dkva_ref[:, 0:HEAD_DIM], dkva_ref[:, HEAD_DIM : 2 * HEAD_DIM]
        dk = dk * SCALE
        low = jnp.where(left, dk, pltpu.roll(dv, half, 1))
        high = jnp.where(left, pltpu.roll(dk, half, 1), dv)
        send_ref[rows, :] = jnp.where(side == 0, high, low).astype(jnp.bfloat16)
        kept = jnp.where(side == 0, low, high)
        if n < BACK:
            far_ref[rows, :] = kept.astype(jnp.bfloat16)
        else:
            own_ref[...] = kept


def finish_kernel(info, mine12, mine3, theirs12, theirs3, own_ref, r1_ref, r2_ref, r3_ref,
                  out_ref, key_ref, value_ref, sems):
    for s in range(3):
        source = info[8 + s]
        dst = out_ref.at[pl.ds(s * BLOCK, BLOCK), :]

        def copy(src, s=s, dst=dst):
            return pltpu.make_async_copy(src, dst, sems.at[s])

        for number, array in enumerate((mine12, theirs12)):
            @pl.when((source == 3 * number) | (source == 3 * number + 1))
            def _(array=array, number=number, source=source, copy=copy):
                row = pl.multiple_of(jnp.clip(source - 3 * number, 0, 1) * BLOCK, BLOCK)
                copy(array.at[pl.ds(row, BLOCK), :]).start()
        for number, array in enumerate((mine3, theirs3)):
            @pl.when(source == 3 * number + 2)
            def _(array=array, copy=copy):
                copy(array).start()
    total = own_ref[...]
    for ref in (r1_ref, r2_ref, r3_ref):
        total = total + ref[...].astype(jnp.float32)
    half = HEAD_DIM // 2
    for n in range(total.shape[0] // BLOCK):
        lanes = slice(n * BLOCK, (n + 1) * BLOCK)
        turned = total[lanes, :].T.astype(jnp.bfloat16)
        key_ref[:, lanes] = turned[:half]
        value_ref[:, lanes] = turned[half:]
    for s in range(3):
        pltpu.make_async_copy(mine3, out_ref.at[pl.ds(s * BLOCK, BLOCK), :], sems.at[s]).wait()


def on_device(queries, key_states, value_states, attn_out, grad_out, log_norm, lengths, block_plan):
    tokens, feature = queries.shape
    heads = feature // HEAD_DIM
    blocks = tokens // BLOCK
    half_axis = lax.axis_size("seq") // 2
    window = BACK * tokens
    kv_group = lax.axis_index("head") // 2
    own_kv = jnp.concatenate([
        lax.dynamic_slice_in_dim(key_states, kv_group * HEAD_DIM, HEAD_DIM, 1),
        lax.dynamic_slice_in_dim(value_states, kv_group * HEAD_DIM, HEAD_DIM, 1)], axis=1)
    kv3, kv2, kv1 = (shifted(own_kv, "seq", n) for n in (3, 2, 1))

    f32, bf16, i32 = jnp.float32, jnp.bfloat16, jnp.int32
    queries, attn_out, grad_out, log_norm, lengths, block_plan = (
        pltpu.with_memory_space_constraint(a, pltpu.HBM)
        for a in (queries, attn_out, grad_out, log_norm, lengths, block_plan))
    smem = pl.BlockSpec(memory_space=pltpu.SMEM)
    vmem = pl.BlockSpec(memory_space=pltpu.VMEM)
    hbm = pl.BlockSpec(memory_space=pltpu.HBM)
    params = pltpu.CompilerParams(vmem_limit_bytes=VMEM_LIMIT)
    own_dq, own_dkv, rows, starts, qs, dos, info, branch = pl.pallas_call(
        functools.partial(own_kernel, heads, half_axis),
        in_specs=[smem, smem, vmem, hbm, hbm, hbm, vmem],
        out_specs=[vmem] * 6 + [smem] * 2,
        out_shape=[pltpu.VMEM((tokens, feature), f32),
                   pltpu.VMEM((tokens, 2 * HEAD_DIM), f32),
                   pltpu.VMEM((blocks, 16, BLOCK), f32),
                   pltpu.VMEM((blocks, 8, BLOCK), i32),
                   pltpu.VMEM((blocks * feature, HEAD_DIM), bf16),
                   pltpu.VMEM((blocks * feature, HEAD_DIM), bf16),
                   jax.ShapeDtypeStruct((16,), i32),
                   jax.ShapeDtypeStruct((1,), i32)],
        scratch_shapes=[pltpu.VMEM((tokens, feature), bf16)] * 3 + [pltpu.SemaphoreType.DMA((blocks, 3))],
        compiler_params=params,
        cost_estimate=pl.CostEstimate(flops=2_000_000_000, bytes_accessed=4_000_000, transcendentals=600_000),
        name="own_keys",
    )(lengths, block_plan, own_kv, queries, attn_out, grad_out, log_norm)

    dq12, dq3, send, far, own = pl.pallas_call(
        functools.partial(rest_kernel, heads),
        in_specs=[smem] + [vmem] * 9,
        out_specs=[vmem] * 5,
        out_shape=[pltpu.VMEM((2 * BLOCK, feature), bf16),
                   pltpu.VMEM((BLOCK, feature), bf16),
                   pltpu.VMEM((window + tokens, HEAD_DIM), bf16),
                   pltpu.VMEM((window, HEAD_DIM), bf16),
                   pltpu.VMEM((tokens, HEAD_DIM), f32)],
        scratch_shapes=[pltpu.VMEM((BLOCK, feature), f32),
                        pltpu.VMEM((window, 2 * HEAD_DIM), bf16), pltpu.VMEM((window, 2 * HEAD_DIM), f32)],
        compiler_params=params,
        cost_estimate=pl.CostEstimate(flops=2_000_000_000, bytes_accessed=4_000_000, transcendentals=600_000),
        name="rest_keys",
    )(info, starts, kv3, kv2, kv1, qs, dos, rows, own_dq, own_dkv)

    theirs12 = swapped(dq12, "seq", half_axis)

    def returns(mask, dq3, send, far, own):
        pairs = [(i, i ^ half_axis) for i in range(2 * half_axis) if mask >> (i % half_axis % GROUPS) & 1]
        theirs3 = lax.ppermute(dq3, "seq", pairs) if pairs else dq3
        arrived = swapped(send, "head", 1).astype(f32)
        both = (far.astype(f32) + arrived[:window]).astype(bf16)
        back = [shifted(both[(BACK - n) * tokens : (BACK - n + 1) * tokens], "seq", -n) for n in (3, 2, 1)]
        return (theirs3, own + arrived[window:], *back)

    branches = [functools.partial(returns, mask) for mask in range(1 << GROUPS)]
    theirs3, own, back3, back2, back1 = lax.switch(branch.reshape(()), branches, dq3, send, far, own)

    grad_half = jax.ShapeDtypeStruct((HEAD_DIM // 2, tokens), bf16)
    query_grad, key_grad, value_grad = pl.pallas_call(
        finish_kernel,
        in_specs=[smem] + [vmem] * 8,
        out_specs=[hbm, vmem, vmem],
        out_shape=[jax.ShapeDtypeStruct((tokens, feature), bf16), grad_half, grad_half],
        scratch_shapes=[pltpu.SemaphoreType.DMA((3,))],
        compiler_params=params,
        name="place_blocks",
    )(info, dq12, dq3, theirs12, theirs3, own, back1, back2, back3)
    return query_grad, key_grad.T, value_grad.T


def solution(mesh):
    placed = (
        P("seq", "head"),
        P("seq", None),
        P("seq", None),
        P("seq", "head"),
        P("seq", "head"),
        P("head", "seq"),
        P(),
        P(),
    )
    return jax.shard_map(
        on_device,
        mesh=mesh,
        in_specs=placed,
        out_specs=(P("seq", "head"), P("seq", "head"), P("seq", "head")),
        check_vma=False,
    )
```

```python
import functools

import jax
import jax.numpy as jnp
from jax import lax
from jax.experimental import pallas as pl
from jax.experimental.pallas import tpu as pltpu
from jax.sharding import PartitionSpec as P

HEAD_DIM = 128
BLOCK = 128
BACK = 3
VMEM_LIMIT = 20 * 2**20
GROUPS = 4
LOG2E = 1.4426950408889634
SCALE = HEAD_DIM ** -0.5


def shifted(value, axis, steps):
    count = lax.axis_size(axis)
    first, last = (max(0, -steps), min(count, count - steps))
    return lax.ppermute(value, axis, [(i, i + steps) for i in range(first, last)])


def swapped(array, axis, apart):
    return lax.ppermute(array, axis, [(i, i ^ apart) for i in range(lax.axis_size(axis))])


def dot(a, b):
    return jnp.dot(a, b, preferred_element_type=jnp.float32)


def dot_nt(a, b):
    return lax.dot_general(a, b, (((1,), (1,)), ((), ())), preferred_element_type=jnp.float32)


def tile_grads(kt, vt, qs, dos, rows, allowed, heads):
    scores = dot_nt(kt, qs)
    prob_grad = dot_nt(vt, dos)
    weights, score_grads = [], []
    for h in range(heads):
        cols = slice(h * BLOCK, (h + 1) * BLOCK)
        lse = rows[h : h + 1, :]
        delta = rows[heads + h : heads + h + 1, :]
        w = jnp.where(allowed, jnp.exp2(scores[:, cols] * (SCALE * LOG2E) - lse), 0.0)
        weights.append(w.astype(jnp.bfloat16))
        score_grads.append((w * (prob_grad[:, cols] - delta)).astype(jnp.bfloat16))
    w_half = jnp.concatenate(weights, axis=1)
    s_grad = jnp.concatenate(score_grads, axis=1)
    dv = dot(w_half, dos)
    dk = dot(s_grad, qs)
    dq_t = dot(kt.T, s_grad)
    return dq_t, dk, dv


def plan_info(info_ref, branch_ref, lengths_ref, plan_ref, device, half_axis, side, per_device):
    first = device * per_device
    partner = device ^ half_axis
    locals_ = range(per_device)
    theirs = [plan_ref[partner * per_device + s] for s in locals_]
    mine = [plan_ref[first + s] for s in locals_]
    ranks = []
    for l in locals_:
        rank = per_device + l
        for s in locals_:
            rank = jnp.where(theirs[s] == first + l, s, rank)
        ranks.append(rank)
    position = [sum((ranks[m] < ranks[l]).astype(jnp.int32) for m in locals_ if m != l) for l in locals_]
    starts = [jnp.int32(0)] * per_device
    begin = jnp.int32(0)
    for n in range(lengths_ref.shape[0]):
        starts = [jnp.where(begin <= (first + l) * BLOCK, begin, starts[l]) for l in locals_]
        begin = begin + lengths_ref[n]
    info_ref[0] = device
    info_ref[1] = side
    for i in locals_:
        info_ref[2 + i] = sum(jnp.where(position[l] == i, l, 0) for l in locals_)
        info_ref[5 + i] = sum(jnp.where(position[l] == i, starts[l], 0) for l in locals_)
    far_rank = jnp.int32(0)
    for s in locals_:
        local = mine[s] - first
        near = (local >= 0) & (local < per_device)
        near_position = sum(jnp.where(local == l, position[l], 0) for l in locals_)
        info_ref[8 + s] = jnp.where(near, near_position, per_device + far_rank)
        far_rank = far_rank + jnp.where(near, 0, 1)
    mask = jnp.int32(0)
    for pair in range(half_axis):
        full = jnp.bool_(True)
        for s in locals_:
            local = plan_ref[pair * per_device + s] - pair * per_device
            full = full & ((local < 0) | (local >= per_device))
        mask = mask | jnp.where(full, 1 << (pair * GROUPS // half_axis), 0)
    branch_ref[0] = mask
    return starts


def own_kernel(heads, half_axis, lengths_ref, plan_ref, kv_ref, kv1_ref, q_hbm, o_hbm, do_hbm, lse_ref,
               dq_ref, dkv_ref, rows_ref, starts_ref, qs_ref, dos_ref, info_ref, branch_ref,
               q_buf, o_buf, do_buf, sems):
    tokens = kv_ref.shape[0]
    blocks = tokens // BLOCK
    feature = heads * HEAD_DIM

    def copies(j):
        rows = pl.ds(j * BLOCK, BLOCK)
        pairs = ((do_hbm, do_buf), (o_hbm, o_buf), (q_hbm, q_buf))
        return [pltpu.make_async_copy(a.at[rows, :], b.at[rows, :], sems.at[j, n]) for n, (a, b) in enumerate(pairs)]

    for j in range(blocks):
        for c in copies(j):
            c.start()
    device = lax.axis_index("seq")
    base = device * tokens
    dkv_ref[...] = jnp.zeros_like(dkv_ref)
    first_starts = plan_info(info_ref, branch_ref, lengths_ref, plan_ref, device, half_axis, lax.axis_index("head") & 1, blocks)

    pos = base + lax.broadcasted_iota(jnp.int32, (1, tokens), 1)
    start = jnp.zeros((1, tokens), jnp.int32)
    begin = jnp.int32(0)
    for n in range(lengths_ref.shape[0]):
        start = jnp.where(pos >= begin, begin, start)
        begin = begin + lengths_ref[n]

    ones = jnp.ones((8, 2 * HEAD_DIM), jnp.bfloat16)
    for j in range(blocks):
        rows = pl.ds(j * BLOCK, BLOCK)
        lanes = slice(j * BLOCK, (j + 1) * BLOCK)
        for c in copies(j):
            c.wait()
        for h in range(heads):
            cols = pl.ds(h * HEAD_DIM, HEAD_DIM)
            stacked = pl.ds(j * feature + h * HEAD_DIM, HEAD_DIM)
            qs_ref[stacked, :] = q_buf[rows, cols]
            dos_ref[stacked, :] = do_buf[rows, cols]
            prod = do_buf[rows, cols].astype(jnp.float32) * o_buf[rows, cols].astype(jnp.float32)
            high = prod.astype(jnp.bfloat16)
            low = (prod - high.astype(jnp.float32)).astype(jnp.bfloat16)
            row = dot_nt(ones, jnp.concatenate([high, low], axis=1))
            rows_ref[j, heads + h : heads + h + 1, :] = row[0:1, :]
        rows_ref[j, 0:heads, :] = lse_ref[:, lanes].astype(jnp.float32) * LOG2E
        start_row, pos_row = start[:, lanes], pos[:, lanes]
        starts_ref[j] = jnp.broadcast_to(start_row, (8, BLOCK))
        keys = slice(0, (j + 1) * BLOCK)
        queries = pl.ds(j * feature, feature)
        key_pos = base + lax.broadcasted_iota(jnp.int32, ((j + 1) * BLOCK, BLOCK), 0)
        allowed = (key_pos >= start_row) & (key_pos <= pos_row)
        dq_t, dk, dv = tile_grads(kv_ref[keys, 0:HEAD_DIM], kv_ref[keys, HEAD_DIM : 2 * HEAD_DIM],
                                  qs_ref[queries, :], dos_ref[queries, :], rows_ref.at[j], allowed, heads)
        dq_ref[rows, :] = dq_t
        mine = pl.ds(tokens, (j + 1) * BLOCK)
        dkv_ref[mine, 0:HEAD_DIM] += dk
        dkv_ref[mine, HEAD_DIM : 2 * HEAD_DIM] += dv

        @pl.when(first_starts[j] < base)
        def _(j=j, rows=rows, queries=queries, start_row=start_row):
            key_pos = base - tokens + lax.broadcasted_iota(jnp.int32, (tokens, BLOCK), 0)
            dq_t, dk, dv = tile_grads(kv1_ref[:, 0:HEAD_DIM], kv1_ref[:, HEAD_DIM : 2 * HEAD_DIM],
                                      qs_ref[queries, :], dos_ref[queries, :], rows_ref.at[j],
                                      key_pos >= start_row, heads)
            dq_ref[rows, :] += dq_t
            dkv_ref[pl.ds(0, tokens), 0:HEAD_DIM] += dk
            dkv_ref[pl.ds(0, tokens), HEAD_DIM : 2 * HEAD_DIM] += dv


def block_rest(i, heads, info, starts_ref, kv_ref, qs_ref, dos_ref, rows_ref, dqa_ref, dkv_ref, dq_ref, out_ref, row=0):
    tokens = dqa_ref.shape[0]
    feature = heads * HEAD_DIM
    blocks = tokens // BLOCK
    base = (info[0] - BACK) * tokens
    block = jnp.clip(info[2 + i], 0, blocks - 1)
    first = jnp.clip(lax.div(info[5 + i] - base, tokens), 0, BACK - 1)
    queries = pl.ds(pl.multiple_of(block * feature, feature), feature)
    dq_ref[...] = dqa_ref[pl.ds(pl.multiple_of(block * BLOCK, BLOCK), BLOCK), :]
    start_row = starts_ref[block, 0:1, :]

    def step(t, carry):
        keys = pl.ds(pl.multiple_of(t * tokens, tokens), tokens)
        key_pos = base + t * tokens + lax.broadcasted_iota(jnp.int32, (tokens, BLOCK), 0)
        dq_t, dk, dv = tile_grads(kv_ref[keys, 0:HEAD_DIM], kv_ref[keys, HEAD_DIM : 2 * HEAD_DIM],
                                  qs_ref[queries, :], dos_ref[queries, :], rows_ref.at[block],
                                  key_pos >= start_row, heads)
        dq_ref[...] += dq_t
        dkv_ref[keys, 0:HEAD_DIM] += dk
        dkv_ref[keys, HEAD_DIM : 2 * HEAD_DIM] += dv
        return carry

    lax.fori_loop(first, BACK - 1, step, 0)
    for h in range(heads):
        cols = pl.ds(h * HEAD_DIM, HEAD_DIM)
        out_ref[pl.ds(row, BLOCK), cols] = (dq_ref[:, cols].T * SCALE).astype(jnp.bfloat16)


def first_kernel(heads, info, starts_ref, kv2_ref, kv3_ref, qs_ref, dos_ref, rows_ref, dqa_ref,
                 out_ref, kv_ref, dkv_ref, dq_ref):
    tokens = kv3_ref.shape[0]
    dkv_ref[...] = jnp.zeros_like(dkv_ref)
    for n, ref in enumerate((kv3_ref, kv2_ref)):
        kv_ref[pl.ds(n * tokens, tokens), :] = ref[...]
    for i in range(2):
        block_rest(i, heads, info, starts_ref, kv_ref, qs_ref, dos_ref, rows_ref, dqa_ref, dkv_ref, dq_ref, out_ref,
                   i * BLOCK)


def rest_kernel(heads, info, starts_ref, kv_ref, qs_ref, dos_ref, rows_ref, dqa_ref, dkva_ref, dkvb_ref,
                third_ref, send_ref, far_ref, own_ref, dq_ref, dkv_ref):
    tokens = dkva_ref.shape[0] // 2
    dkv_ref[...] = dkvb_ref[...]
    block_rest(2, heads, info, starts_ref, kv_ref, qs_ref, dos_ref, rows_ref, dqa_ref, dkv_ref, dq_ref, third_ref)

    side = info[1]
    half = HEAD_DIM // 2
    left = lax.broadcasted_iota(jnp.int32, (tokens, HEAD_DIM), 1) < half
    for n in range(BACK + 1):
        rows = pl.ds(n * tokens, tokens)
        ref, first = (dkv_ref, n * tokens) if n < BACK - 1 else (dkva_ref, (n - BACK + 1) * tokens)
        dk = ref[pl.ds(first, tokens), 0:HEAD_DIM] * SCALE
        dv = ref[pl.ds(first, tokens), HEAD_DIM : 2 * HEAD_DIM]
        low = jnp.where(left, dk, pltpu.roll(dv, half, 1))
        high = jnp.where(left, pltpu.roll(dk, half, 1), dv)
        send_ref[rows, :] = jnp.where(side == 0, high, low).astype(jnp.bfloat16)
        kept = jnp.where(side == 0, low, high)
        if n < BACK:
            far_ref[rows, :] = kept.astype(jnp.bfloat16)
        else:
            own_ref[...] = kept


def place(info, first, pair, single, out_ref, sems, act):
    arrays = (pair.at[pl.ds(0, BLOCK), :], pair.at[pl.ds(BLOCK, BLOCK), :], single)
    for s in range(3):
        for number, array in enumerate(arrays):
            @pl.when(info[8 + s] == first + number)
            def _(array=array, s=s):
                getattr(pltpu.make_async_copy(array, out_ref.at[pl.ds(s * BLOCK, BLOCK), :], sems.at[s]), act)()


def keep_kernel(info, mine12, mine3, out_ref, sems):
    place(info, 0, mine12, mine3, out_ref, sems, "start")
    place(info, 0, mine12, mine3, out_ref, sems, "wait")


def finish_kernel(info, theirs12, theirs3, own_ref, mate_ref, r2_ref, r3_ref, placed_ref,
                  out_ref, key_ref, value_ref, sems):
    place(info, 3, theirs12, theirs3, out_ref, sems, "start")
    total = own_ref[...] + r2_ref[...].astype(jnp.float32) + r3_ref[...].astype(jnp.float32)
    tokens = total.shape[0]
    total = total + jnp.where(lax.rem(info[0], 2) == 0, mate_ref[tokens:, :].astype(jnp.float32), 0.0)
    half = HEAD_DIM // 2
    for n in range(total.shape[0] // BLOCK):
        lanes = slice(n * BLOCK, (n + 1) * BLOCK)
        turned = total[lanes, :].T.astype(jnp.bfloat16)
        key_ref[:, lanes] = turned[:half]
        value_ref[:, lanes] = turned[half:]
    place(info, 3, theirs12, theirs3, out_ref, sems, "wait")


def on_device(queries, key_states, value_states, attn_out, grad_out, log_norm, lengths, block_plan):
    tokens, feature = queries.shape
    heads = feature // HEAD_DIM
    blocks = tokens // BLOCK
    half_axis = lax.axis_size("seq") // 2
    window = BACK * tokens
    kv_group = lax.axis_index("head") // 2
    own_kv = jnp.concatenate([
        lax.dynamic_slice_in_dim(key_states, kv_group * HEAD_DIM, HEAD_DIM, 1),
        lax.dynamic_slice_in_dim(value_states, kv_group * HEAD_DIM, HEAD_DIM, 1)], axis=1)
    devices = 2 * half_axis
    kv1, kv2, kv3 = (shifted(own_kv, "seq", n) for n in (1, 2, 3))
    later = (BACK - 1) * tokens
    f32, bf16, i32 = jnp.float32, jnp.bfloat16, jnp.int32
    queries, attn_out, grad_out, log_norm, lengths, block_plan = (
        pltpu.with_memory_space_constraint(a, pltpu.HBM)
        for a in (queries, attn_out, grad_out, log_norm, lengths, block_plan))
    smem = pl.BlockSpec(memory_space=pltpu.SMEM)
    vmem = pl.BlockSpec(memory_space=pltpu.VMEM)
    hbm = pl.BlockSpec(memory_space=pltpu.HBM)
    params = pltpu.CompilerParams(vmem_limit_bytes=VMEM_LIMIT)
    own_dq, own_dkv, rows, starts, qs, dos, info, branch = pl.pallas_call(
        functools.partial(own_kernel, heads, half_axis),
        in_specs=[smem, smem, vmem, vmem, hbm, hbm, hbm, vmem],
        out_specs=[vmem] * 6 + [smem] * 2,
        out_shape=[pltpu.VMEM((tokens, feature), f32),
                   pltpu.VMEM((2 * tokens, 2 * HEAD_DIM), f32),
                   pltpu.VMEM((blocks, 16, BLOCK), f32),
                   pltpu.VMEM((blocks, 8, BLOCK), i32),
                   pltpu.VMEM((blocks * feature, HEAD_DIM), bf16),
                   pltpu.VMEM((blocks * feature, HEAD_DIM), bf16),
                   jax.ShapeDtypeStruct((16,), i32),
                   jax.ShapeDtypeStruct((1,), i32)],
        scratch_shapes=[pltpu.VMEM((tokens, feature), bf16)] * 3 + [pltpu.SemaphoreType.DMA((blocks, 3))],
        compiler_params=params,
        cost_estimate=pl.CostEstimate(flops=2_000_000_000, bytes_accessed=4_000_000, transcendentals=600_000),
        name="own_keys",
    )(lengths, block_plan, own_kv, kv1, queries, attn_out, grad_out, log_norm)

    cost = pl.CostEstimate(flops=1_000, bytes_accessed=1_000, transcendentals=0)
    dq12, kv, dkv = pl.pallas_call(
        functools.partial(first_kernel, heads),
        in_specs=[smem] + [vmem] * 7,
        out_specs=[vmem] * 3,
        out_shape=[pltpu.VMEM((2 * BLOCK, feature), bf16),
                   pltpu.VMEM((later, 2 * HEAD_DIM), bf16),
                   pltpu.VMEM((later, 2 * HEAD_DIM), f32)],
        scratch_shapes=[pltpu.VMEM((BLOCK, feature), f32)],
        compiler_params=params,
        cost_estimate=cost,
        name="first_blocks",
    )(info, starts, kv2, kv3, qs, dos, rows, own_dq)
    theirs12 = swapped(dq12, "seq", half_axis)

    dq3, send, far, own = pl.pallas_call(
        functools.partial(rest_kernel, heads),
        in_specs=[smem] + [vmem] * 8,
        out_specs=[vmem] * 4,
        out_shape=[pltpu.VMEM((BLOCK, feature), bf16),
                   pltpu.VMEM((window + tokens, HEAD_DIM), bf16),
                   pltpu.VMEM((window, HEAD_DIM), bf16),
                   pltpu.VMEM((tokens, HEAD_DIM), f32)],
        scratch_shapes=[pltpu.VMEM((BLOCK, feature), f32), pltpu.VMEM((later, 2 * HEAD_DIM), f32)],
        compiler_params=params,
        cost_estimate=cost,
        name="last_block",
    )(info, starts, kv, qs, dos, rows, own_dq, own_dkv, dkv)

    def returns(mask, dq3, send, far, own):
        pairs = [(i, i ^ half_axis) for i in range(2 * half_axis) if mask >> (i % half_axis * GROUPS // half_axis) & 1]
        theirs3 = lax.ppermute(dq3, "seq", pairs) if pairs else dq3
        arrived = swapped(send, "head", 1).astype(f32)
        third, second, first = ((far[n * tokens : (n + 1) * tokens].astype(f32)
                                 + arrived[n * tokens : (n + 1) * tokens]).astype(bf16) for n in range(BACK))
        odd = lax.axis_index("seq") % 2 == 1
        mate = swapped(jnp.concatenate([jnp.where(odd, third, first), first], axis=0), "seq", 1)
        back3 = lax.ppermute(third, "seq", [(i, i - 3) for i in range(4, devices, 2)])
        back2 = shifted((second.astype(f32) + mate[:tokens].astype(f32)).astype(bf16), "seq", -2)
        return (theirs3, own + arrived[window:], mate, back2, back3)

    branches = [functools.partial(returns, mask) for mask in range(1 << GROUPS)]
    theirs3, own, mate, back2, back3 = lax.switch(branch.reshape(()), branches, dq3, send, far, own)

    grad_half = jax.ShapeDtypeStruct((HEAD_DIM // 2, tokens), bf16)
    whole = jax.ShapeDtypeStruct((tokens, feature), bf16)
    copy_sems = [pltpu.SemaphoreType.DMA((3,))]
    placed = pl.pallas_call(
        keep_kernel,
        in_specs=[smem, vmem, vmem],
        out_specs=hbm,
        out_shape=whole,
        scratch_shapes=copy_sems,
        compiler_params=params,
        name="keep_blocks",
    )(info, dq12, dq3)
    query_grad, key_grad, value_grad = pl.pallas_call(
        finish_kernel,
        in_specs=[smem] + [vmem] * 6 + [hbm],
        out_specs=[hbm, vmem, vmem],
        out_shape=[whole, grad_half, grad_half],
        input_output_aliases={7: 0},
        scratch_shapes=copy_sems,
        compiler_params=params,
        name="place_blocks",
    )(info, theirs12, theirs3, own, mate, back2, back3, placed)
    return query_grad, key_grad.T, value_grad.T


def solution(mesh):
    placed = (
        P("seq", "head"),
        P("seq", None),
        P("seq", None),
        P("seq", "head"),
        P("seq", "head"),
        P("head", "seq"),
        P(),
        P(),
    )
    return jax.shard_map(
        on_device,
        mesh=mesh,
        in_specs=placed,
        out_specs=(P("seq", "head"), P("seq", "head"), P("seq", "head")),
        check_vma=False,
    )
```

```python
import functools

import jax
import jax.numpy as jnp
from jax import lax
from jax.experimental import pallas as pl
from jax.experimental.pallas import tpu as pltpu
from jax.sharding import PartitionSpec as P

HEAD_DIM = 128
BLOCK = 128
BACK = 3
VMEM_LIMIT = 20 * 2**20
GROUPS = 4
LOG2E = 1.4426950408889634
SCALE = HEAD_DIM ** -0.5


def shifted(value, axis, steps):
    count = lax.axis_size(axis)
    first, last = (max(0, -steps), min(count, count - steps))
    return lax.ppermute(value, axis, [(i, i + steps) for i in range(first, last)])


def swapped(array, axis, apart):
    return lax.ppermute(array, axis, [(i, i ^ apart) for i in range(lax.axis_size(axis))])


def dot(a, b):
    return jnp.dot(a, b, preferred_element_type=jnp.float32)


def dot_nt(a, b):
    return lax.dot_general(a, b, (((1,), (1,)), ((), ())), preferred_element_type=jnp.float32)


def tile_grads(kt, vt, qs, dos, rows, allowed, heads):
    scores = dot_nt(kt, qs)
    prob_grad = dot_nt(vt, dos)
    weights, score_grads = [], []
    for h in range(heads):
        cols = slice(h * BLOCK, (h + 1) * BLOCK)
        lse = rows[h : h + 1, :]
        delta = rows[heads + h : heads + h + 1, :]
        w = jnp.where(allowed, jnp.exp2(scores[:, cols] * (SCALE * LOG2E) - lse), 0.0)
        weights.append(w.astype(jnp.bfloat16))
        score_grads.append((w * (prob_grad[:, cols] - delta)).astype(jnp.bfloat16))
    w_half = jnp.concatenate(weights, axis=1)
    s_grad = jnp.concatenate(score_grads, axis=1)
    dv = dot(w_half, dos)
    dk = dot(s_grad, qs)
    dq_t = dot(kt.T, s_grad)
    return dq_t, dk, dv


def plan_info(info_ref, branch_ref, lengths_ref, plan_ref, device, half_axis, side, per_device):
    first = device * per_device
    partner = device ^ half_axis
    locals_ = range(per_device)
    theirs = [plan_ref[partner * per_device + s] for s in locals_]
    mine = [plan_ref[first + s] for s in locals_]
    ranks = []
    for l in locals_:
        rank = per_device + l
        for s in locals_:
            rank = jnp.where(theirs[s] == first + l, s, rank)
        ranks.append(rank)
    position = [sum((ranks[m] < ranks[l]).astype(jnp.int32) for m in locals_ if m != l) for l in locals_]
    starts = [jnp.int32(0)] * per_device
    begin = jnp.int32(0)
    for n in range(lengths_ref.shape[0]):
        starts = [jnp.where(begin <= (first + l) * BLOCK, begin, starts[l]) for l in locals_]
        begin = begin + lengths_ref[n]
    info_ref[0] = device
    info_ref[1] = side
    for i in locals_:
        info_ref[2 + i] = sum(jnp.where(position[l] == i, l, 0) for l in locals_)
        info_ref[5 + i] = sum(jnp.where(position[l] == i, starts[l], 0) for l in locals_)
    far_rank = jnp.int32(0)
    for s in locals_:
        local = mine[s] - first
        near = (local >= 0) & (local < per_device)
        near_position = sum(jnp.where(local == l, position[l], 0) for l in locals_)
        info_ref[8 + s] = jnp.where(near, near_position, per_device + far_rank)
        far_rank = far_rank + jnp.where(near, 0, 1)
    mask = jnp.int32(0)
    for pair in range(half_axis):
        full = jnp.bool_(True)
        for s in locals_:
            local = plan_ref[pair * per_device + s] - pair * per_device
            full = full & ((local < 0) | (local >= per_device))
        mask = mask | jnp.where(full, 1 << (pair * GROUPS // half_axis), 0)
    branch_ref[0] = mask


def prepare_kernel(heads, half_axis, lengths_ref, plan_ref, q_hbm, o_hbm, do_hbm, lse_ref,
                   rows_ref, starts_ref, qs_ref, dos_ref, info_ref, branch_ref, q_buf, o_buf, do_buf, sems):
    tokens = q_buf.shape[0]
    blocks = tokens // BLOCK
    feature = heads * HEAD_DIM

    def copies(j):
        rows = pl.ds(j * BLOCK, BLOCK)
        pairs = ((do_hbm, do_buf), (o_hbm, o_buf), (q_hbm, q_buf))
        return [pltpu.make_async_copy(a.at[rows, :], b.at[rows, :], sems.at[j, n]) for n, (a, b) in enumerate(pairs)]

    for j in range(blocks):
        for c in copies(j):
            c.start()
    device = lax.axis_index("seq")
    plan_info(info_ref, branch_ref, lengths_ref, plan_ref, device, half_axis, lax.axis_index("head") & 1, blocks)

    pos = device * tokens + lax.broadcasted_iota(jnp.int32, (1, tokens), 1)
    start = jnp.zeros((1, tokens), jnp.int32)
    begin = jnp.int32(0)
    for n in range(lengths_ref.shape[0]):
        start = jnp.where(pos >= begin, begin, start)
        begin = begin + lengths_ref[n]

    ones = jnp.ones((8, 2 * HEAD_DIM), jnp.bfloat16)
    for j in range(blocks):
        rows = pl.ds(j * BLOCK, BLOCK)
        lanes = slice(j * BLOCK, (j + 1) * BLOCK)
        starts_ref[j] = jnp.broadcast_to(start[:, lanes], (8, BLOCK))
        rows_ref[j, 0:heads, :] = lse_ref[:, lanes].astype(jnp.float32) * LOG2E
        for c in copies(j):
            c.wait()
        for h in range(heads):
            cols = pl.ds(h * HEAD_DIM, HEAD_DIM)
            stacked = pl.ds(j * feature + h * HEAD_DIM, HEAD_DIM)
            qs_ref[stacked, :] = q_buf[rows, cols]
            dos_ref[stacked, :] = do_buf[rows, cols]
            prod = do_buf[rows, cols].astype(jnp.float32) * o_buf[rows, cols].astype(jnp.float32)
            high = prod.astype(jnp.bfloat16)
            low = (prod - high.astype(jnp.float32)).astype(jnp.bfloat16)
            row = dot_nt(ones, jnp.concatenate([high, low], axis=1))
            rows_ref[j, heads + h : heads + h + 1, :] = row[0:1, :]


def own_kernel(heads, info, starts_ref, kv_ref, qs_ref, dos_ref, rows_ref, dq_ref, dkv_ref):
    tokens = kv_ref.shape[0]
    feature = heads * HEAD_DIM
    base = info[0] * tokens
    dkv_ref[...] = jnp.zeros_like(dkv_ref)
    for j in range(tokens // BLOCK):
        rows = pl.ds(j * BLOCK, BLOCK)
        keys = slice(0, (j + 1) * BLOCK)
        queries = pl.ds(j * feature, feature)
        pos_row = base + j * BLOCK + lax.broadcasted_iota(jnp.int32, (1, BLOCK), 1)
        key_pos = base + lax.broadcasted_iota(jnp.int32, ((j + 1) * BLOCK, BLOCK), 0)
        allowed = (key_pos >= starts_ref[j, 0:1, :]) & (key_pos <= pos_row)
        dq_t, dk, dv = tile_grads(kv_ref[keys, 0:HEAD_DIM], kv_ref[keys, HEAD_DIM : 2 * HEAD_DIM],
                                  qs_ref[queries, :], dos_ref[queries, :], rows_ref.at[j], allowed, heads)
        dq_ref[rows, :] = dq_t
        dkv_ref[keys, 0:HEAD_DIM] += dk
        dkv_ref[keys, HEAD_DIM : 2 * HEAD_DIM] += dv


def block_rest(i, heads, info, starts_ref, kv_ref, qs_ref, dos_ref, rows_ref, dqa_ref, dkv_ref, dq_ref, out_ref, row=0):
    tokens = dqa_ref.shape[0]
    feature = heads * HEAD_DIM
    blocks = tokens // BLOCK
    base = (info[0] - BACK) * tokens
    block = jnp.clip(info[2 + i], 0, blocks - 1)
    first = jnp.clip(lax.div(info[5 + i] - base, tokens), 0, BACK)
    queries = pl.ds(pl.multiple_of(block * feature, feature), feature)
    dq_ref[...] = dqa_ref[pl.ds(pl.multiple_of(block * BLOCK, BLOCK), BLOCK), :]
    start_row = starts_ref[block, 0:1, :]

    def step(t, carry):
        keys = pl.ds(pl.multiple_of(t * tokens, tokens), tokens)
        key_pos = base + t * tokens + lax.broadcasted_iota(jnp.int32, (tokens, BLOCK), 0)
        dq_t, dk, dv = tile_grads(kv_ref[keys, 0:HEAD_DIM], kv_ref[keys, HEAD_DIM : 2 * HEAD_DIM],
                                  qs_ref[queries, :], dos_ref[queries, :], rows_ref.at[block],
                                  key_pos >= start_row, heads)
        dq_ref[...] += dq_t
        dkv_ref[keys, 0:HEAD_DIM] += dk
        dkv_ref[keys, HEAD_DIM : 2 * HEAD_DIM] += dv
        return carry

    lax.fori_loop(first, BACK, step, 0)
    for h in range(heads):
        cols = pl.ds(h * HEAD_DIM, HEAD_DIM)
        out_ref[pl.ds(row, BLOCK), cols] = (dq_ref[:, cols].T * SCALE).astype(jnp.bfloat16)


def first_kernel(heads, info, starts_ref, mate_ref, chip_ref, far_ref, qs_ref, dos_ref, rows_ref, dqa_ref,
                 out_ref, kv_ref, dkv_ref, dq_ref):
    tokens = chip_ref.shape[0]
    dkv_ref[...] = jnp.zeros_like(dkv_ref)
    kv_ref[pl.ds(tokens, tokens), :] = chip_ref[...]
    odd = lax.rem(info[0], 2)
    for parity, (third_back, one_back) in enumerate(((far_ref, mate_ref), (mate_ref, far_ref))):
        @pl.when(odd == parity)
        def _(third_back=third_back, one_back=one_back):
            kv_ref[pl.ds(0, tokens), :] = third_back[...]
            kv_ref[pl.ds(2 * tokens, tokens), :] = one_back[...]

    for i in range(2):
        block_rest(i, heads, info, starts_ref, kv_ref, qs_ref, dos_ref, rows_ref, dqa_ref, dkv_ref, dq_ref, out_ref,
                   i * BLOCK)


def rest_kernel(heads, info, starts_ref, kv_ref, qs_ref, dos_ref, rows_ref, dqa_ref, dkva_ref, dkvb_ref,
                third_ref, send_ref, far_ref, own_ref, dq_ref, dkv_ref):
    tokens = dkva_ref.shape[0]
    dkv_ref[...] = dkvb_ref[...]
    block_rest(2, heads, info, starts_ref, kv_ref, qs_ref, dos_ref, rows_ref, dqa_ref, dkv_ref, dq_ref, third_ref)

    side = info[1]
    half = HEAD_DIM // 2
    left = lax.broadcasted_iota(jnp.int32, (tokens, HEAD_DIM), 1) < half
    for n in range(BACK + 1):
        rows = pl.ds(n * tokens, tokens)
        ref, first = (dkv_ref, n * tokens) if n < BACK else (dkva_ref, 0)
        dk = ref[pl.ds(first, tokens), 0:HEAD_DIM] * SCALE
        dv = ref[pl.ds(first, tokens), HEAD_DIM : 2 * HEAD_DIM]
        low = jnp.where(left, dk, pltpu.roll(dv, half, 1))
        high = jnp.where(left, pltpu.roll(dk, half, 1), dv)
        send_ref[rows, :] = jnp.where(side == 0, high, low).astype(jnp.bfloat16)
        kept = jnp.where(side == 0, low, high)
        if n < BACK:
            far_ref[rows, :] = kept.astype(jnp.bfloat16)
        else:
            own_ref[...] = kept


def place(info, arrays, out_ref, sems, act):
    for s in range(3):
        for number, array in arrays:
            @pl.when(info[8 + s] == number)
            def _(array=array, s=s):
                getattr(pltpu.make_async_copy(array, out_ref.at[pl.ds(s * BLOCK, BLOCK), :], sems.at[s]), act)()


def both_blocks(first, pair):
    return [(first, pair.at[pl.ds(0, BLOCK), :]), (first + 1, pair.at[pl.ds(BLOCK, BLOCK), :])]


def keep_kernel(info, mine12, mine3, out_ref, sems):
    arrays = both_blocks(0, mine12) + [(2, mine3)]
    place(info, arrays, out_ref, sems, "start")
    place(info, arrays, out_ref, sems, "wait")


def finish_kernel(info, theirs12, theirs3_hbm, own_ref, mate_hbm, r2_hbm, r3_hbm, placed_ref,
                  out_ref, key_ref, value_ref, sems, theirs3, mate_ref, r2_ref, r3_ref):
    tokens = own_ref.shape[0]
    pairs = ((mate_hbm.at[pl.ds(tokens, tokens), :], mate_ref), (r2_hbm, r2_ref), (r3_hbm, r3_ref))
    loads = [pltpu.make_async_copy(a, b, sems.at[3 + n]) for n, (a, b) in enumerate(pairs)]
    for load in loads:
        load.start()
    place(info, both_blocks(3, theirs12), out_ref, sems, "start")
    has_third = (info[8] == 5) | (info[9] == 5) | (info[10] == 5)

    @pl.when(has_third)
    def _():
        load = pltpu.make_async_copy(theirs3_hbm, theirs3, sems.at[6])
        load.start()
        load.wait()
        place(info, [(5, theirs3)], out_ref, sems, "start")

    for load in loads:
        load.wait()
    total = own_ref[...] + r2_ref[...].astype(jnp.float32) + r3_ref[...].astype(jnp.float32)
    total = total + jnp.where(lax.rem(info[0], 2) == 0, mate_ref[...].astype(jnp.float32), 0.0)
    half = HEAD_DIM // 2
    for n in range(total.shape[0] // BLOCK):
        lanes = slice(n * BLOCK, (n + 1) * BLOCK)
        turned = total[lanes, :].T.astype(jnp.bfloat16)
        key_ref[:, lanes] = turned[:half]
        value_ref[:, lanes] = turned[half:]
    place(info, both_blocks(3, theirs12) + [(5, theirs3)], out_ref, sems, "wait")


def on_device(queries, key_states, value_states, attn_out, grad_out, log_norm, lengths, block_plan):
    tokens, feature = queries.shape
    heads = feature // HEAD_DIM
    blocks = tokens // BLOCK
    half_axis = lax.axis_size("seq") // 2
    window = BACK * tokens
    kv_group = lax.axis_index("head") // 2
    own_kv = jnp.concatenate([
        lax.dynamic_slice_in_dim(key_states, kv_group * HEAD_DIM, HEAD_DIM, 1),
        lax.dynamic_slice_in_dim(value_states, kv_group * HEAD_DIM, HEAD_DIM, 1)], axis=1)
    devices = 2 * half_axis
    chip_kv = shifted(own_kv, "seq", 2)
    later = BACK * tokens
    f32, bf16, i32 = jnp.float32, jnp.bfloat16, jnp.int32
    queries, attn_out, grad_out, log_norm, lengths, block_plan = (
        pltpu.with_memory_space_constraint(a, pltpu.HBM)
        for a in (queries, attn_out, grad_out, log_norm, lengths, block_plan))
    smem = pl.BlockSpec(memory_space=pltpu.SMEM)
    vmem = pl.BlockSpec(memory_space=pltpu.VMEM)
    hbm = pl.BlockSpec(memory_space=pltpu.HBM)
    anywhere = pl.BlockSpec(memory_space=pl.ANY)
    params = pltpu.CompilerParams(vmem_limit_bytes=VMEM_LIMIT)
    cost = pl.CostEstimate(flops=1_000, bytes_accessed=1_000, transcendentals=0)
    rows, starts, qs, dos, info, branch = pl.pallas_call(
        functools.partial(prepare_kernel, heads, half_axis),
        in_specs=[smem, smem, hbm, hbm, hbm, vmem],
        out_specs=[vmem] * 4 + [smem] * 2,
        out_shape=[pltpu.VMEM((blocks, 16, BLOCK), f32),
                   pltpu.VMEM((blocks, 8, BLOCK), i32),
                   pltpu.VMEM((blocks * feature, HEAD_DIM), bf16),
                   pltpu.VMEM((blocks * feature, HEAD_DIM), bf16),
                   jax.ShapeDtypeStruct((16,), i32),
                   jax.ShapeDtypeStruct((1,), i32)],
        scratch_shapes=[pltpu.VMEM((tokens, feature), bf16)] * 3 + [pltpu.SemaphoreType.DMA((blocks, 3))],
        compiler_params=params,
        cost_estimate=cost,
        name="prepare",
    )(lengths, block_plan, queries, attn_out, grad_out, log_norm)

    early_kv, chip_kv, rows = lax.optimization_barrier((own_kv, chip_kv, rows))
    far_kv = lax.ppermute(early_kv, "seq", [(i, i + 3 if i % 2 else i + 1) for i in range(devices) if i + 3 < devices or not i % 2])
    mate_kv = swapped(chip_kv, "seq", 1)
    own_dq, own_dkv = pl.pallas_call(
        functools.partial(own_kernel, heads),
        in_specs=[smem] + [vmem] * 5,
        out_specs=[vmem] * 2,
        out_shape=[pltpu.VMEM((tokens, feature), f32), pltpu.VMEM((tokens, 2 * HEAD_DIM), f32)],
        compiler_params=params,
        cost_estimate=cost,
        name="own_keys",
    )(info, starts, own_kv, qs, dos, rows)

    dq12, kv, dkv = pl.pallas_call(
        functools.partial(first_kernel, heads),
        in_specs=[smem] + [vmem] * 8,
        out_specs=[vmem] * 3,
        out_shape=[pltpu.VMEM((2 * BLOCK, feature), bf16),
                   pltpu.VMEM((later, 2 * HEAD_DIM), bf16),
                   pltpu.VMEM((later, 2 * HEAD_DIM), f32)],
        scratch_shapes=[pltpu.VMEM((BLOCK, feature), f32)],
        compiler_params=params,
        cost_estimate=cost,
        name="first_blocks",
    )(info, starts, mate_kv, chip_kv, far_kv, qs, dos, rows, own_dq)
    theirs12 = swapped(dq12, "seq", half_axis)

    dq3, send, far, own = pl.pallas_call(
        functools.partial(rest_kernel, heads),
        in_specs=[smem] + [vmem] * 8,
        out_specs=[vmem] * 4,
        out_shape=[pltpu.VMEM((BLOCK, feature), bf16),
                   pltpu.VMEM((window + tokens, HEAD_DIM), bf16),
                   pltpu.VMEM((window, HEAD_DIM), bf16),
                   pltpu.VMEM((tokens, HEAD_DIM), f32)],
        scratch_shapes=[pltpu.VMEM((BLOCK, feature), f32), pltpu.VMEM((later, 2 * HEAD_DIM), f32)],
        compiler_params=params,
        cost_estimate=cost,
        name="last_block",
    )(info, starts, kv, qs, dos, rows, own_dq, own_dkv, dkv)

    def returns(mask, dq3, send, far, own):
        pairs = [(i, i ^ half_axis) for i in range(2 * half_axis) if mask >> (i % half_axis * GROUPS // half_axis) & 1]
        theirs3 = lax.ppermute(dq3, "seq", pairs) if pairs else dq3
        arrived = swapped(send, "head", 1).astype(f32)
        third, second, first = ((far[n * tokens : (n + 1) * tokens].astype(f32)
                                 + arrived[n * tokens : (n + 1) * tokens]).astype(bf16) for n in range(BACK))
        odd = lax.axis_index("seq") % 2 == 1
        mate = swapped(jnp.concatenate([jnp.where(odd, third, first), first], axis=0), "seq", 1)
        back3 = lax.ppermute(third, "seq", [(i, i - 3) for i in range(4, devices, 2)])
        back2 = shifted((second.astype(f32) + mate[:tokens].astype(f32)).astype(bf16), "seq", -2)
        return (theirs3, own + arrived[window:], mate, back2, back3)

    branches = [functools.partial(returns, mask) for mask in range(1 << GROUPS)]
    theirs3, own, mate, back2, back3 = lax.switch(branch.reshape(()), branches, dq3, send, far, own)

    grad_half = jax.ShapeDtypeStruct((HEAD_DIM // 2, tokens), bf16)
    whole = jax.ShapeDtypeStruct((tokens, feature), bf16)
    copy_sems = [pltpu.SemaphoreType.DMA((3,))]
    placed = pl.pallas_call(
        keep_kernel,
        in_specs=[smem, vmem, vmem],
        out_specs=hbm,
        out_shape=whole,
        scratch_shapes=copy_sems,
        compiler_params=params,
        name="keep_blocks",
    )(info, dq12, dq3)
    query_grad, key_grad, value_grad = pl.pallas_call(
        finish_kernel,
        in_specs=[smem, vmem, anywhere, vmem] + [anywhere] * 3 + [hbm],
        out_specs=[hbm, vmem, vmem],
        out_shape=[whole, grad_half, grad_half],
        input_output_aliases={7: 0},
        scratch_shapes=[pltpu.SemaphoreType.DMA((7,)), pltpu.VMEM((BLOCK, feature), bf16)]
        + [pltpu.VMEM((tokens, HEAD_DIM), bf16)] * 3,
        compiler_params=params,
        name="place_blocks",
    )(info, theirs12, theirs3, own, mate, back2, back3, placed)
    return query_grad, key_grad.T, value_grad.T


def solution(mesh):
    placed = (
        P("seq", "head"),
        P("seq", None),
        P("seq", None),
        P("seq", "head"),
        P("seq", "head"),
        P("head", "seq"),
        P(),
        P(),
    )
    return jax.shard_map(
        on_device,
        mesh=mesh,
        in_specs=placed,
        out_specs=(P("seq", "head"), P("seq", "head"), P("seq", "head")),
        check_vma=False,
    )
```

```python
import functools

import jax
import jax.numpy as jnp
from jax import lax
from jax.experimental import pallas as pl
from jax.experimental.pallas import tpu as pltpu
from jax.sharding import PartitionSpec as P

HEAD_DIM = 128
BLOCK = 128
BACK = 3
VMEM_LIMIT = 20 * 2**20
GROUPS = 4
LOG2E = 1.4426950408889634
SCALE = HEAD_DIM ** -0.5


def shifted(value, axis, steps):
    count = lax.axis_size(axis)
    first, last = (max(0, -steps), min(count, count - steps))
    return lax.ppermute(value, axis, [(i, i + steps) for i in range(first, last)])


def swapped(array, axis, apart):
    return lax.ppermute(array, axis, [(i, i ^ apart) for i in range(lax.axis_size(axis))])


def dot(a, b):
    return jnp.dot(a, b, preferred_element_type=jnp.float32)


def dot_nt(a, b):
    return lax.dot_general(a, b, (((1,), (1,)), ((), ())), preferred_element_type=jnp.float32)


def tile_grads(kt, vt, qs, dos, rows, allowed, heads):
    scores = dot_nt(kt, qs)
    prob_grad = dot_nt(vt, dos)
    weights, score_grads = [], []
    for h in range(heads):
        cols = slice(h * BLOCK, (h + 1) * BLOCK)
        lse = rows[h : h + 1, :]
        delta = rows[heads + h : heads + h + 1, :]
        w = jnp.where(allowed, jnp.exp2(scores[:, cols] * (SCALE * LOG2E) - lse), 0.0)
        weights.append(w.astype(jnp.bfloat16))
        score_grads.append((w * (prob_grad[:, cols] - delta)).astype(jnp.bfloat16))
    w_half = jnp.concatenate(weights, axis=1)
    s_grad = jnp.concatenate(score_grads, axis=1)
    dv = dot(w_half, dos)
    dk = dot(s_grad, qs)
    dq_t = dot(kt.T, s_grad)
    return dq_t, dk, dv


def plan_info(info_ref, branch_ref, lengths_ref, plan_ref, device, half_axis, side, per_device):
    first = device * per_device
    partner = device ^ half_axis
    locals_ = range(per_device)
    theirs = [plan_ref[partner * per_device + s] for s in locals_]
    mine = [plan_ref[first + s] for s in locals_]
    ranks = []
    for l in locals_:
        rank = per_device + l
        for s in locals_:
            rank = jnp.where(theirs[s] == first + l, s, rank)
        ranks.append(rank)
    position = [sum((ranks[m] < ranks[l]).astype(jnp.int32) for m in locals_ if m != l) for l in locals_]
    starts = [jnp.int32(0)] * per_device
    begin = jnp.int32(0)
    for n in range(lengths_ref.shape[0]):
        starts = [jnp.where(begin <= (first + l) * BLOCK, begin, starts[l]) for l in locals_]
        begin = begin + lengths_ref[n]
    info_ref[0] = device
    info_ref[1] = side
    for i in locals_:
        info_ref[2 + i] = sum(jnp.where(position[l] == i, l, 0) for l in locals_)
        info_ref[5 + i] = sum(jnp.where(position[l] == i, starts[l], 0) for l in locals_)
    far_rank = jnp.int32(0)
    for s in locals_:
        local = mine[s] - first
        near = (local >= 0) & (local < per_device)
        near_position = sum(jnp.where(local == l, position[l], 0) for l in locals_)
        info_ref[8 + s] = jnp.where(near, near_position, per_device + far_rank)
        far_rank = far_rank + jnp.where(near, 0, 1)
    mask = jnp.int32(0)
    for pair in range(half_axis):
        full = jnp.bool_(True)
        for s in locals_:
            local = plan_ref[pair * per_device + s] - pair * per_device
            full = full & ((local < 0) | (local >= per_device))
        mask = mask | jnp.where(full, 1 << (pair * GROUPS // half_axis), 0)
    branch_ref[0] = mask


def prepare_kernel(heads, half_axis, lengths_ref, plan_ref, q_hbm, o_hbm, do_hbm, lse_ref,
                   rows_ref, starts_ref, qs_ref, dos_ref, info_ref, branch_ref, q_buf, o_buf, do_buf, sems):
    tokens = q_buf.shape[0]
    blocks = tokens // BLOCK
    feature = heads * HEAD_DIM

    def copies(j):
        rows = pl.ds(j * BLOCK, BLOCK)
        pairs = ((do_hbm, do_buf), (o_hbm, o_buf), (q_hbm, q_buf))
        return [pltpu.make_async_copy(a.at[rows, :], b.at[rows, :], sems.at[j, n]) for n, (a, b) in enumerate(pairs)]

    for j in range(blocks):
        for c in copies(j):
            c.start()
    device = lax.axis_index("seq")
    plan_info(info_ref, branch_ref, lengths_ref, plan_ref, device, half_axis, lax.axis_index("head") & 1, blocks)

    pos = device * tokens + lax.broadcasted_iota(jnp.int32, (1, tokens), 1)
    start = jnp.zeros((1, tokens), jnp.int32)
    begin = jnp.int32(0)
    for n in range(lengths_ref.shape[0]):
        start = jnp.where(pos >= begin, begin, start)
        begin = begin + lengths_ref[n]

    ones = jnp.ones((8, 2 * HEAD_DIM), jnp.bfloat16)
    for j in range(blocks):
        rows = pl.ds(j * BLOCK, BLOCK)
        lanes = slice(j * BLOCK, (j + 1) * BLOCK)
        starts_ref[j] = jnp.broadcast_to(start[:, lanes], (8, BLOCK))
        rows_ref[j, 0:heads, :] = lse_ref[:, lanes].astype(jnp.float32) * LOG2E
        for c in copies(j):
            c.wait()
        for h in range(heads):
            cols = pl.ds(h * HEAD_DIM, HEAD_DIM)
            stacked = pl.ds(j * feature + h * HEAD_DIM, HEAD_DIM)
            qs_ref[stacked, :] = q_buf[rows, cols]
            dos_ref[stacked, :] = do_buf[rows, cols]
            prod = do_buf[rows, cols].astype(jnp.float32) * o_buf[rows, cols].astype(jnp.float32)
            high = prod.astype(jnp.bfloat16)
            low = (prod - high.astype(jnp.float32)).astype(jnp.bfloat16)
            row = dot_nt(ones, jnp.concatenate([high, low], axis=1))
            rows_ref[j, heads + h : heads + h + 1, :] = row[0:1, :]


def own_kernel(heads, info, starts_ref, kv_ref, qs_ref, dos_ref, rows_ref, dq_ref, dkv_ref):
    tokens = kv_ref.shape[0]
    feature = heads * HEAD_DIM
    base = info[0] * tokens
    dkv_ref[...] = jnp.zeros_like(dkv_ref)
    for j in range(tokens // BLOCK):
        rows = pl.ds(j * BLOCK, BLOCK)
        keys = slice(0, (j + 1) * BLOCK)
        queries = pl.ds(j * feature, feature)
        pos_row = base + j * BLOCK + lax.broadcasted_iota(jnp.int32, (1, BLOCK), 1)
        key_pos = base + lax.broadcasted_iota(jnp.int32, ((j + 1) * BLOCK, BLOCK), 0)
        allowed = (key_pos >= starts_ref[j, 0:1, :]) & (key_pos <= pos_row)
        dq_t, dk, dv = tile_grads(kv_ref[keys, 0:HEAD_DIM], kv_ref[keys, HEAD_DIM : 2 * HEAD_DIM],
                                  qs_ref[queries, :], dos_ref[queries, :], rows_ref.at[j], allowed, heads)
        dq_ref[rows, :] = dq_t
        dkv_ref[keys, 0:HEAD_DIM] += dk
        dkv_ref[keys, HEAD_DIM : 2 * HEAD_DIM] += dv


def block_rest(i, heads, info, starts_ref, kv_ref, qs_ref, dos_ref, rows_ref, dqa_ref, dkv_ref, dq_ref, out_ref, row=0):
    tokens = dqa_ref.shape[0]
    feature = heads * HEAD_DIM
    blocks = tokens // BLOCK
    base = (info[0] - BACK) * tokens
    block = jnp.clip(info[2 + i], 0, blocks - 1)
    first = jnp.clip(lax.div(info[5 + i] - base, tokens), 0, BACK)
    queries = pl.ds(pl.multiple_of(block * feature, feature), feature)
    dq_ref[...] = dqa_ref[pl.ds(pl.multiple_of(block * BLOCK, BLOCK), BLOCK), :]
    start_row = starts_ref[block, 0:1, :]

    def step(t, carry):
        keys = pl.ds(pl.multiple_of(t * tokens, tokens), tokens)
        key_pos = base + t * tokens + lax.broadcasted_iota(jnp.int32, (tokens, BLOCK), 0)
        dq_t, dk, dv = tile_grads(kv_ref[keys, 0:HEAD_DIM], kv_ref[keys, HEAD_DIM : 2 * HEAD_DIM],
                                  qs_ref[queries, :], dos_ref[queries, :], rows_ref.at[block],
                                  key_pos >= start_row, heads)
        dq_ref[...] += dq_t
        dkv_ref[keys, 0:HEAD_DIM] += dk
        dkv_ref[keys, HEAD_DIM : 2 * HEAD_DIM] += dv
        return carry

    lax.fori_loop(first, BACK, step, 0)
    for h in range(heads):
        cols = pl.ds(h * HEAD_DIM, HEAD_DIM)
        out_ref[pl.ds(row, BLOCK), cols] = (dq_ref[:, cols].T * SCALE).astype(jnp.bfloat16)


def first_kernel(heads, info, starts_ref, mate_ref, chip_ref, far_ref, qs_ref, dos_ref, rows_ref, dqa_ref,
                 out_ref, kv_ref, dkv_ref, dq_ref):
    tokens = chip_ref.shape[0]
    dkv_ref[...] = jnp.zeros_like(dkv_ref)
    kv_ref[pl.ds(tokens, tokens), :] = chip_ref[...]
    odd = lax.rem(info[0], 2)
    for parity, (third_back, one_back) in enumerate(((far_ref, mate_ref), (mate_ref, far_ref))):
        @pl.when(odd == parity)
        def _(third_back=third_back, one_back=one_back):
            kv_ref[pl.ds(0, tokens), :] = third_back[...]
            kv_ref[pl.ds(2 * tokens, tokens), :] = one_back[...]

    for i in range(2):
        block_rest(i, heads, info, starts_ref, kv_ref, qs_ref, dos_ref, rows_ref, dqa_ref, dkv_ref, dq_ref, out_ref,
                   i * BLOCK)


def rest_kernel(heads, info, starts_ref, kv_ref, qs_ref, dos_ref, rows_ref, dqa_ref, dkva_ref, dkvb_ref,
                third_ref, send_ref, far_ref, own_ref, dq_ref, dkv_ref):
    tokens = dkva_ref.shape[0]
    dkv_ref[...] = dkvb_ref[...]
    block_rest(2, heads, info, starts_ref, kv_ref, qs_ref, dos_ref, rows_ref, dqa_ref, dkv_ref, dq_ref, third_ref)

    side = info[1]
    half = HEAD_DIM // 2
    left = lax.broadcasted_iota(jnp.int32, (tokens, HEAD_DIM), 1) < half
    for n in range(BACK + 1):
        rows = pl.ds(n * tokens, tokens)
        ref, first = (dkv_ref, n * tokens) if n < BACK else (dkva_ref, 0)
        dk = ref[pl.ds(first, tokens), 0:HEAD_DIM] * SCALE
        dv = ref[pl.ds(first, tokens), HEAD_DIM : 2 * HEAD_DIM]
        low = jnp.where(left, dk, pltpu.roll(dv, half, 1))
        high = jnp.where(left, pltpu.roll(dk, half, 1), dv)
        send_ref[rows, :] = jnp.where(side == 0, high, low).astype(jnp.bfloat16)
        kept = jnp.where(side == 0, low, high)
        if n < BACK:
            far_ref[rows, :] = kept.astype(jnp.bfloat16)
        else:
            own_ref[...] = kept


def place(info, arrays, out_ref, sems, act):
    for s in range(3):
        for number, array in arrays:
            @pl.when(info[8 + s] == number)
            def _(array=array, s=s):
                getattr(pltpu.make_async_copy(array, out_ref.at[pl.ds(s * BLOCK, BLOCK), :], sems.at[s]), act)()


def both_blocks(first, pair):
    return [(first, pair.at[pl.ds(0, BLOCK), :]), (first + 1, pair.at[pl.ds(BLOCK, BLOCK), :])]


def keep_kernel(info, mine12, mine3, out_ref, sems):
    arrays = both_blocks(0, mine12) + [(2, mine3)]
    place(info, arrays, out_ref, sems, "start")
    place(info, arrays, out_ref, sems, "wait")


def finish_kernel(info, theirs12, theirs3_hbm, own_ref, r2_hbm, r3_hbm, placed_ref,
                  out_ref, key_ref, value_ref, sems, theirs3, r2_ref, r3_ref):
    pairs = ((r2_hbm, r2_ref), (r3_hbm, r3_ref))
    loads = [pltpu.make_async_copy(a, b, sems.at[3 + n]) for n, (a, b) in enumerate(pairs)]
    for load in loads:
        load.start()
    place(info, both_blocks(3, theirs12), out_ref, sems, "start")
    has_third = (info[8] == 5) | (info[9] == 5) | (info[10] == 5)

    @pl.when(has_third)
    def _():
        load = pltpu.make_async_copy(theirs3_hbm, theirs3, sems.at[6])
        load.start()
        load.wait()
        place(info, [(5, theirs3)], out_ref, sems, "start")

    for load in loads:
        load.wait()
    total = own_ref[...] + r2_ref[...].astype(jnp.float32) + r3_ref[...].astype(jnp.float32)
    half = HEAD_DIM // 2
    for n in range(total.shape[0] // BLOCK):
        lanes = slice(n * BLOCK, (n + 1) * BLOCK)
        turned = total[lanes, :].T.astype(jnp.bfloat16)
        key_ref[:, lanes] = turned[:half]
        value_ref[:, lanes] = turned[half:]
    place(info, both_blocks(3, theirs12) + [(5, theirs3)], out_ref, sems, "wait")


def on_device(queries, key_states, value_states, attn_out, grad_out, log_norm, lengths, block_plan):
    tokens, feature = queries.shape
    heads = feature // HEAD_DIM
    blocks = tokens // BLOCK
    half_axis = lax.axis_size("seq") // 2
    window = BACK * tokens
    kv_group = lax.axis_index("head") // 2
    own_kv = jnp.concatenate([
        lax.dynamic_slice_in_dim(key_states, kv_group * HEAD_DIM, HEAD_DIM, 1),
        lax.dynamic_slice_in_dim(value_states, kv_group * HEAD_DIM, HEAD_DIM, 1)], axis=1)
    devices = 2 * half_axis
    chip_kv = shifted(own_kv, "seq", 2)
    far_kv = lax.ppermute(own_kv, "seq", [(i, i + 3 if i % 2 else i + 1) for i in range(devices) if i + 3 < devices or not i % 2])
    later = BACK * tokens
    f32, bf16, i32 = jnp.float32, jnp.bfloat16, jnp.int32
    queries, attn_out, grad_out, log_norm, lengths, block_plan = (
        pltpu.with_memory_space_constraint(a, pltpu.HBM)
        for a in (queries, attn_out, grad_out, log_norm, lengths, block_plan))
    smem = pl.BlockSpec(memory_space=pltpu.SMEM)
    vmem = pl.BlockSpec(memory_space=pltpu.VMEM)
    hbm = pl.BlockSpec(memory_space=pltpu.HBM)
    anywhere = pl.BlockSpec(memory_space=pl.ANY)
    params = pltpu.CompilerParams(vmem_limit_bytes=VMEM_LIMIT)
    cost = pl.CostEstimate(flops=1_000, bytes_accessed=1_000, transcendentals=0)
    rows, starts, qs, dos, info, branch = pl.pallas_call(
        functools.partial(prepare_kernel, heads, half_axis),
        in_specs=[smem, smem, hbm, hbm, hbm, vmem],
        out_specs=[vmem] * 4 + [smem] * 2,
        out_shape=[pltpu.VMEM((blocks, 16, BLOCK), f32),
                   pltpu.VMEM((blocks, 8, BLOCK), i32),
                   pltpu.VMEM((blocks * feature, HEAD_DIM), bf16),
                   pltpu.VMEM((blocks * feature, HEAD_DIM), bf16),
                   jax.ShapeDtypeStruct((16,), i32),
                   jax.ShapeDtypeStruct((1,), i32)],
        scratch_shapes=[pltpu.VMEM((tokens, feature), bf16)] * 3 + [pltpu.SemaphoreType.DMA((blocks, 3))],
        compiler_params=params,
        cost_estimate=cost,
        name="prepare",
    )(lengths, block_plan, queries, attn_out, grad_out, log_norm)

    chip_kv, rows = lax.optimization_barrier((chip_kv, rows))
    mate_kv = swapped(chip_kv, "seq", 1)
    own_dq, own_dkv = pl.pallas_call(
        functools.partial(own_kernel, heads),
        in_specs=[smem] + [vmem] * 5,
        out_specs=[vmem] * 2,
        out_shape=[pltpu.VMEM((tokens, feature), f32), pltpu.VMEM((tokens, 2 * HEAD_DIM), f32)],
        compiler_params=params,
        cost_estimate=cost,
        name="own_keys",
    )(info, starts, own_kv, qs, dos, rows)

    dq12, kv, dkv = pl.pallas_call(
        functools.partial(first_kernel, heads),
        in_specs=[smem] + [vmem] * 8,
        out_specs=[vmem] * 3,
        out_shape=[pltpu.VMEM((2 * BLOCK, feature), bf16),
                   pltpu.VMEM((later, 2 * HEAD_DIM), bf16),
                   pltpu.VMEM((later, 2 * HEAD_DIM), f32)],
        scratch_shapes=[pltpu.VMEM((BLOCK, feature), f32)],
        compiler_params=params,
        cost_estimate=cost,
        name="first_blocks",
    )(info, starts, mate_kv, chip_kv, far_kv, qs, dos, rows, own_dq)
    theirs12 = swapped(dq12, "seq", half_axis)

    dq3, send, far, own = pl.pallas_call(
        functools.partial(rest_kernel, heads),
        in_specs=[smem] + [vmem] * 8,
        out_specs=[vmem] * 4,
        out_shape=[pltpu.VMEM((BLOCK, feature), bf16),
                   pltpu.VMEM((window + tokens, HEAD_DIM), bf16),
                   pltpu.VMEM((window, HEAD_DIM), bf16),
                   pltpu.VMEM((tokens, HEAD_DIM), f32)],
        scratch_shapes=[pltpu.VMEM((BLOCK, feature), f32), pltpu.VMEM((later, 2 * HEAD_DIM), f32)],
        compiler_params=params,
        cost_estimate=cost,
        name="last_block",
    )(info, starts, kv, qs, dos, rows, own_dq, own_dkv, dkv)

    def returns(mask, dq3, send, far, own):
        pairs = [(i, i ^ half_axis) for i in range(2 * half_axis) if mask >> (i % half_axis * GROUPS // half_axis) & 1]
        theirs3 = lax.ppermute(dq3, "seq", pairs) if pairs else dq3
        odd = lax.axis_index("seq") % 2 == 1
        halves = jnp.concatenate([send[:window], far], axis=1)
        third, second, first = (halves[n * tokens : (n + 1) * tokens] for n in range(BACK))
        mate = swapped(jnp.concatenate([jnp.where(odd, third, first), first], axis=0), "seq", 1).astype(f32)
        second = second.astype(f32) + mate[:tokens]
        mine = jnp.where(odd, 0.0, mate[tokens:])
        own = own + mine[:, HEAD_DIM:]
        sent = send[window:].astype(f32) + mine[:, :HEAD_DIM]
        arrived = swapped(jnp.concatenate([second[:, :HEAD_DIM].astype(bf16), sent.astype(bf16), send[:tokens]], axis=0),
                          "head", 1).astype(f32)
        back3 = lax.ppermute((far[:tokens].astype(f32) + arrived[2 * tokens :]).astype(bf16), "seq",
                             [(i, i - 3) for i in range(4, devices, 2)])
        back2 = shifted((second[:, HEAD_DIM:] + arrived[:tokens]).astype(bf16), "seq", -2)
        return (theirs3, own + arrived[tokens : 2 * tokens], back2, back3)

    branches = [functools.partial(returns, mask) for mask in range(1 << GROUPS)]
    theirs3, own, back2, back3 = lax.switch(branch.reshape(()), branches, dq3, send, far, own)

    grad_half = jax.ShapeDtypeStruct((HEAD_DIM // 2, tokens), bf16)
    whole = jax.ShapeDtypeStruct((tokens, feature), bf16)
    copy_sems = [pltpu.SemaphoreType.DMA((3,))]
    placed = pl.pallas_call(
        keep_kernel,
        in_specs=[smem, vmem, vmem],
        out_specs=hbm,
        out_shape=whole,
        scratch_shapes=copy_sems,
        compiler_params=params,
        name="keep_blocks",
    )(info, dq12, dq3)
    query_grad, key_grad, value_grad = pl.pallas_call(
        finish_kernel,
        in_specs=[smem, vmem, anywhere, vmem] + [anywhere] * 2 + [hbm],
        out_specs=[hbm, vmem, vmem],
        out_shape=[whole, grad_half, grad_half],
        input_output_aliases={6: 0},
        scratch_shapes=[pltpu.SemaphoreType.DMA((7,)), pltpu.VMEM((BLOCK, feature), bf16)]
        + [pltpu.VMEM((tokens, HEAD_DIM), bf16)] * 2,
        compiler_params=params,
        name="place_blocks",
    )(info, theirs12, theirs3, own, back2, back3, placed)
    return query_grad, key_grad.T, value_grad.T


def solution(mesh):
    placed = (
        P("seq", "head"),
        P("seq", None),
        P("seq", None),
        P("seq", "head"),
        P("seq", "head"),
        P("head", "seq"),
        P(),
        P(),
    )
    return jax.shard_map(
        on_device,
        mesh=mesh,
        in_specs=placed,
        out_specs=(P("seq", "head"), P("seq", "head"), P("seq", "head")),
        check_vma=False,
    )
```

```python
import functools

import jax
import jax.numpy as jnp
from jax import lax
from jax.experimental import pallas as pl
from jax.experimental.pallas import tpu as pltpu
from jax.sharding import PartitionSpec as P

HEAD_DIM = 128
BLOCK = 128
BACK = 3
VMEM_LIMIT = 20 * 2**20
GROUPS = 4
LOG2E = 1.4426950408889634
SCALE = HEAD_DIM ** -0.5


def shifted(value, axis, steps):
    count = lax.axis_size(axis)
    first, last = (max(0, -steps), min(count, count - steps))
    return lax.ppermute(value, axis, [(i, i + steps) for i in range(first, last)])


def swapped(array, axis, apart):
    return lax.ppermute(array, axis, [(i, i ^ apart) for i in range(lax.axis_size(axis))])


def dot(a, b):
    return jnp.dot(a, b, preferred_element_type=jnp.float32)


def dot_nt(a, b):
    return lax.dot_general(a, b, (((1,), (1,)), ((), ())), preferred_element_type=jnp.float32)


def tile_grads(kt, vt, qs, dos, rows, allowed, heads):
    scores = dot_nt(kt, qs)
    prob_grad = dot_nt(vt, dos)
    weights, score_grads = [], []
    for h in range(heads):
        cols = slice(h * BLOCK, (h + 1) * BLOCK)
        lse = rows[h : h + 1, :]
        delta = rows[heads + h : heads + h + 1, :]
        w = jnp.where(allowed, jnp.exp2(scores[:, cols] * (SCALE * LOG2E) - lse), 0.0)
        weights.append(w.astype(jnp.bfloat16))
        score_grads.append((w * (prob_grad[:, cols] - delta)).astype(jnp.bfloat16))
    w_half = jnp.concatenate(weights, axis=1)
    s_grad = jnp.concatenate(score_grads, axis=1)
    dv = dot(w_half, dos)
    dk = dot(s_grad, qs)
    dq_t = dot(kt.T, s_grad)
    return dq_t, dk, dv


def plan_info(info_ref, branch_ref, lengths_ref, plan_ref, device, half_axis, side, per_device):
    first = device * per_device
    partner = device ^ half_axis
    locals_ = range(per_device)
    theirs = [plan_ref[partner * per_device + s] for s in locals_]
    mine = [plan_ref[first + s] for s in locals_]
    ranks = []
    for l in locals_:
        rank = per_device + l
        for s in locals_:
            rank = jnp.where(theirs[s] == first + l, s, rank)
        ranks.append(rank)
    position = [sum((ranks[m] < ranks[l]).astype(jnp.int32) for m in locals_ if m != l) for l in locals_]
    starts = [jnp.int32(0)] * per_device
    begin = jnp.int32(0)
    for n in range(lengths_ref.shape[0]):
        starts = [jnp.where(begin <= (first + l) * BLOCK, begin, starts[l]) for l in locals_]
        begin = begin + lengths_ref[n]
    info_ref[0] = device
    info_ref[1] = side
    for i in locals_:
        info_ref[2 + i] = sum(jnp.where(position[l] == i, l, 0) for l in locals_)
        info_ref[5 + i] = sum(jnp.where(position[l] == i, starts[l], 0) for l in locals_)
    far_rank = jnp.int32(0)
    for s in locals_:
        local = mine[s] - first
        near = (local >= 0) & (local < per_device)
        near_position = sum(jnp.where(local == l, position[l], 0) for l in locals_)
        info_ref[8 + s] = jnp.where(near, near_position, per_device + far_rank)
        far_rank = far_rank + jnp.where(near, 0, 1)
    mask = jnp.int32(0)
    for pair in range(half_axis):
        full = jnp.bool_(True)
        for s in locals_:
            local = plan_ref[pair * per_device + s] - pair * per_device
            full = full & ((local < 0) | (local >= per_device))
        mask = mask | jnp.where(full, 1 << (pair * GROUPS // half_axis), 0)
    branch_ref[0] = mask


def prepare_kernel(heads, half_axis, lengths_ref, plan_ref, q_hbm, o_hbm, do_hbm, lse_ref,
                   rows_ref, starts_ref, qs_ref, dos_ref, info_ref, branch_ref, q_buf, o_buf, do_buf, sems):
    tokens = q_buf.shape[0]
    blocks = tokens // BLOCK
    feature = heads * HEAD_DIM

    def copies(j):
        rows = pl.ds(j * BLOCK, BLOCK)
        pairs = ((do_hbm, do_buf), (o_hbm, o_buf), (q_hbm, q_buf))
        return [pltpu.make_async_copy(a.at[rows, :], b.at[rows, :], sems.at[j, n]) for n, (a, b) in enumerate(pairs)]

    for j in range(blocks):
        for c in copies(j):
            c.start()
    device = lax.axis_index("seq")
    plan_info(info_ref, branch_ref, lengths_ref, plan_ref, device, half_axis, lax.axis_index("head") & 1, blocks)

    pos = device * tokens + lax.broadcasted_iota(jnp.int32, (1, tokens), 1)
    start = jnp.zeros((1, tokens), jnp.int32)
    begin = jnp.int32(0)
    for n in range(lengths_ref.shape[0]):
        start = jnp.where(pos >= begin, begin, start)
        begin = begin + lengths_ref[n]

    ones = jnp.ones((8, 2 * HEAD_DIM), jnp.bfloat16)
    for j in range(blocks):
        rows = pl.ds(j * BLOCK, BLOCK)
        lanes = slice(j * BLOCK, (j + 1) * BLOCK)
        starts_ref[j] = jnp.broadcast_to(start[:, lanes], (8, BLOCK))
        rows_ref[j, 0:heads, :] = lse_ref[:, lanes].astype(jnp.float32) * LOG2E
        for c in copies(j):
            c.wait()
        for h in range(heads):
            cols = pl.ds(h * HEAD_DIM, HEAD_DIM)
            stacked = pl.ds(j * feature + h * HEAD_DIM, HEAD_DIM)
            qs_ref[stacked, :] = q_buf[rows, cols]
            dos_ref[stacked, :] = do_buf[rows, cols]
            prod = do_buf[rows, cols].astype(jnp.float32) * o_buf[rows, cols].astype(jnp.float32)
            high = prod.astype(jnp.bfloat16)
            low = (prod - high.astype(jnp.float32)).astype(jnp.bfloat16)
            row = dot_nt(ones, jnp.concatenate([high, low], axis=1))
            rows_ref[j, heads + h : heads + h + 1, :] = row[0:1, :]


def own_kernel(heads, info, starts_ref, kv_ref, qs_ref, dos_ref, rows_ref, dq_ref, dkv_ref):
    tokens = kv_ref.shape[0]
    feature = heads * HEAD_DIM
    base = info[0] * tokens
    dkv_ref[...] = jnp.zeros_like(dkv_ref)
    for j in range(tokens // BLOCK):
        rows = pl.ds(j * BLOCK, BLOCK)
        keys = slice(0, (j + 1) * BLOCK)
        queries = pl.ds(j * feature, feature)
        pos_row = base + j * BLOCK + lax.broadcasted_iota(jnp.int32, (1, BLOCK), 1)
        key_pos = base + lax.broadcasted_iota(jnp.int32, ((j + 1) * BLOCK, BLOCK), 0)
        allowed = (key_pos >= starts_ref[j, 0:1, :]) & (key_pos <= pos_row)
        dq_t, dk, dv = tile_grads(kv_ref[keys, 0:HEAD_DIM], kv_ref[keys, HEAD_DIM : 2 * HEAD_DIM],
                                  qs_ref[queries, :], dos_ref[queries, :], rows_ref.at[j], allowed, heads)
        dq_ref[rows, :] = dq_t
        dkv_ref[keys, 0:HEAD_DIM] += dk
        dkv_ref[keys, HEAD_DIM : 2 * HEAD_DIM] += dv


def block_rest(i, heads, info, starts_ref, kv_ref, qs_ref, dos_ref, rows_ref, dqa_ref, dkv_ref, dq_ref, out_ref, row=0):
    tokens = dqa_ref.shape[0]
    feature = heads * HEAD_DIM
    blocks = tokens // BLOCK
    base = (info[0] - BACK) * tokens
    block = jnp.clip(info[2 + i], 0, blocks - 1)
    first = jnp.clip(lax.div(info[5 + i] - base, tokens), 0, BACK)
    queries = pl.ds(pl.multiple_of(block * feature, feature), feature)
    dq_ref[...] = dqa_ref[pl.ds(pl.multiple_of(block * BLOCK, BLOCK), BLOCK), :]
    start_row = starts_ref[block, 0:1, :]

    def step(t, carry):
        keys = pl.ds(pl.multiple_of(t * tokens, tokens), tokens)
        key_pos = base + t * tokens + lax.broadcasted_iota(jnp.int32, (tokens, BLOCK), 0)
        dq_t, dk, dv = tile_grads(kv_ref[keys, 0:HEAD_DIM], kv_ref[keys, HEAD_DIM : 2 * HEAD_DIM],
                                  qs_ref[queries, :], dos_ref[queries, :], rows_ref.at[block],
                                  key_pos >= start_row, heads)
        dq_ref[...] += dq_t
        dkv_ref[keys, 0:HEAD_DIM] += dk
        dkv_ref[keys, HEAD_DIM : 2 * HEAD_DIM] += dv
        return carry

    lax.fori_loop(first, BACK, step, 0)
    for h in range(heads):
        cols = pl.ds(h * HEAD_DIM, HEAD_DIM)
        out_ref[pl.ds(row, BLOCK), cols] = (dq_ref[:, cols].T * SCALE).astype(jnp.bfloat16)


def first_kernel(heads, info, starts_ref, mate_ref, chip_ref, far_ref, qs_ref, dos_ref, rows_ref, dqa_ref,
                 out_ref, kv_ref, dkv_ref, dq_ref):
    tokens = chip_ref.shape[0]
    dkv_ref[...] = jnp.zeros_like(dkv_ref)
    kv_ref[pl.ds(tokens, tokens), :] = chip_ref[...]
    odd = lax.rem(info[0], 2)
    for parity, (third_back, one_back) in enumerate(((far_ref, mate_ref), (mate_ref, far_ref))):
        @pl.when(odd == parity)
        def _(third_back=third_back, one_back=one_back):
            kv_ref[pl.ds(0, tokens), :] = third_back[...]
            kv_ref[pl.ds(2 * tokens, tokens), :] = one_back[...]

    for i in range(2):
        block_rest(i, heads, info, starts_ref, kv_ref, qs_ref, dos_ref, rows_ref, dqa_ref, dkv_ref, dq_ref, out_ref,
                   i * BLOCK)


def place(info, arrays, out_ref, sems, act):
    for s in range(3):
        for number, array in arrays:
            @pl.when(info[8 + s] == number)
            def _(array=array, s=s):
                getattr(pltpu.make_async_copy(array, out_ref.at[pl.ds(s * BLOCK, BLOCK), :], sems.at[s]), act)()


def both_blocks(first, pair):
    return [(first, pair.at[pl.ds(0, BLOCK), :]), (first + 1, pair.at[pl.ds(BLOCK, BLOCK), :])]


def rest_kernel(heads, info, starts_ref, kv_ref, qs_ref, dos_ref, rows_ref, dqa_ref, dkva_ref, dkvb_ref,
                mine12, third_ref, send_ref, far_ref, own_ref, placed_ref, dq_ref, dkv_ref, sems):
    tokens = dkva_ref.shape[0]
    place(info, both_blocks(0, mine12), placed_ref, sems, "start")
    dkv_ref[...] = dkvb_ref[...]
    block_rest(2, heads, info, starts_ref, kv_ref, qs_ref, dos_ref, rows_ref, dqa_ref, dkv_ref, dq_ref, third_ref)
    place(info, [(2, third_ref)], placed_ref, sems, "start")

    side = info[1]
    half = HEAD_DIM // 2
    left = lax.broadcasted_iota(jnp.int32, (tokens, HEAD_DIM), 1) < half
    for n in range(BACK + 1):
        rows = pl.ds(n * tokens, tokens)
        ref, first = (dkv_ref, n * tokens) if n < BACK else (dkva_ref, 0)
        dk = ref[pl.ds(first, tokens), 0:HEAD_DIM] * SCALE
        dv = ref[pl.ds(first, tokens), HEAD_DIM : 2 * HEAD_DIM]
        low = jnp.where(left, dk, pltpu.roll(dv, half, 1))
        high = jnp.where(left, pltpu.roll(dk, half, 1), dv)
        send_ref[rows, :] = jnp.where(side == 0, high, low).astype(jnp.bfloat16)
        kept = jnp.where(side == 0, low, high)
        if n < BACK:
            far_ref[rows, :] = kept.astype(jnp.bfloat16)
        else:
            own_ref[...] = kept
    place(info, both_blocks(0, mine12) + [(2, third_ref)], placed_ref, sems, "wait")


def finish_kernel(info, theirs12, theirs3_hbm, own_ref, r2_hbm, r3_hbm, placed_ref,
                  out_ref, key_hbm, value_hbm, sems, theirs3, r2_ref, r3_ref, key_ref, value_ref):
    pairs = ((r2_hbm, r2_ref), (r3_hbm, r3_ref))
    loads = [pltpu.make_async_copy(a, b, sems.at[3 + n]) for n, (a, b) in enumerate(pairs)]
    for load in loads:
        load.start()
    place(info, both_blocks(3, theirs12), out_ref, sems, "start")
    has_third = (info[8] == 5) | (info[9] == 5) | (info[10] == 5)

    @pl.when(has_third)
    def _():
        load = pltpu.make_async_copy(theirs3_hbm, theirs3, sems.at[6])
        load.start()
        load.wait()
        place(info, [(5, theirs3)], out_ref, sems, "start")

    for load in loads:
        load.wait()
    total = own_ref[...] + r2_ref[...].astype(jnp.float32) + r3_ref[...].astype(jnp.float32)
    half = HEAD_DIM // 2
    for n in range(total.shape[0] // BLOCK):
        lanes = slice(n * BLOCK, (n + 1) * BLOCK)
        turned = total[lanes, :].T.astype(jnp.bfloat16)
        key_ref[:, lanes] = turned[:half]
        value_ref[:, lanes] = turned[half:]
    stores = [pltpu.make_async_copy(a, b, sems.at[7 + n])
              for n, (a, b) in enumerate(((key_ref, key_hbm), (value_ref, value_hbm)))]
    for store in stores:
        store.start()
    place(info, both_blocks(3, theirs12) + [(5, theirs3)], out_ref, sems, "wait")
    for store in stores:
        store.wait()


def on_device(queries, key_states, value_states, attn_out, grad_out, log_norm, lengths, block_plan):
    tokens, feature = queries.shape
    heads = feature // HEAD_DIM
    blocks = tokens // BLOCK
    half_axis = lax.axis_size("seq") // 2
    window = BACK * tokens
    kv_group = lax.axis_index("head") // 2
    own_kv = jnp.concatenate([
        lax.dynamic_slice_in_dim(key_states, kv_group * HEAD_DIM, HEAD_DIM, 1),
        lax.dynamic_slice_in_dim(value_states, kv_group * HEAD_DIM, HEAD_DIM, 1)], axis=1)
    devices = 2 * half_axis
    chip_kv = shifted(own_kv, "seq", 2)
    far_kv = lax.ppermute(own_kv, "seq", [(i, i + 3 if i % 2 else i + 1) for i in range(devices) if i + 3 < devices or not i % 2])
    later = BACK * tokens
    f32, bf16, i32 = jnp.float32, jnp.bfloat16, jnp.int32
    queries, attn_out, grad_out, log_norm, lengths, block_plan = (
        pltpu.with_memory_space_constraint(a, pltpu.HBM)
        for a in (queries, attn_out, grad_out, log_norm, lengths, block_plan))
    smem = pl.BlockSpec(memory_space=pltpu.SMEM)
    vmem = pl.BlockSpec(memory_space=pltpu.VMEM)
    hbm = pl.BlockSpec(memory_space=pltpu.HBM)
    anywhere = pl.BlockSpec(memory_space=pl.ANY)
    params = pltpu.CompilerParams(vmem_limit_bytes=VMEM_LIMIT)
    cost = pl.CostEstimate(flops=1_000, bytes_accessed=1_000, transcendentals=0)
    rows, starts, qs, dos, info, branch = pl.pallas_call(
        functools.partial(prepare_kernel, heads, half_axis),
        in_specs=[smem, smem, hbm, hbm, hbm, vmem],
        out_specs=[vmem] * 4 + [smem] * 2,
        out_shape=[pltpu.VMEM((blocks, 16, BLOCK), f32),
                   pltpu.VMEM((blocks, 8, BLOCK), i32),
                   pltpu.VMEM((blocks * feature, HEAD_DIM), bf16),
                   pltpu.VMEM((blocks * feature, HEAD_DIM), bf16),
                   jax.ShapeDtypeStruct((16,), i32),
                   jax.ShapeDtypeStruct((1,), i32)],
        scratch_shapes=[pltpu.VMEM((tokens, feature), bf16)] * 3 + [pltpu.SemaphoreType.DMA((blocks, 3))],
        compiler_params=params,
        cost_estimate=cost,
        name="prepare",
    )(lengths, block_plan, queries, attn_out, grad_out, log_norm)

    chip_kv, rows = lax.optimization_barrier((chip_kv, rows))
    mate_kv = swapped(chip_kv, "seq", 1)
    own_dq, own_dkv = pl.pallas_call(
        functools.partial(own_kernel, heads),
        in_specs=[smem] + [vmem] * 5,
        out_specs=[vmem] * 2,
        out_shape=[pltpu.VMEM((tokens, feature), f32), pltpu.VMEM((tokens, 2 * HEAD_DIM), f32)],
        compiler_params=params,
        cost_estimate=cost,
        name="own_keys",
    )(info, starts, own_kv, qs, dos, rows)

    dq12, kv, dkv = pl.pallas_call(
        functools.partial(first_kernel, heads),
        in_specs=[smem] + [vmem] * 8,
        out_specs=[vmem] * 3,
        out_shape=[pltpu.VMEM((2 * BLOCK, feature), bf16),
                   pltpu.VMEM((later, 2 * HEAD_DIM), bf16),
                   pltpu.VMEM((later, 2 * HEAD_DIM), f32)],
        scratch_shapes=[pltpu.VMEM((BLOCK, feature), f32)],
        compiler_params=params,
        cost_estimate=cost,
        name="first_blocks",
    )(info, starts, mate_kv, chip_kv, far_kv, qs, dos, rows, own_dq)
    theirs12 = swapped(dq12, "seq", half_axis)

    dq3, send, far, own, placed = pl.pallas_call(
        functools.partial(rest_kernel, heads),
        in_specs=[smem] + [vmem] * 9,
        out_specs=[vmem] * 4 + [hbm],
        out_shape=[pltpu.VMEM((BLOCK, feature), bf16),
                   pltpu.VMEM((window + tokens, HEAD_DIM), bf16),
                   pltpu.VMEM((window, HEAD_DIM), bf16),
                   pltpu.VMEM((tokens, HEAD_DIM), f32),
                   jax.ShapeDtypeStruct((tokens, feature), bf16)],
        scratch_shapes=[pltpu.VMEM((BLOCK, feature), f32), pltpu.VMEM((later, 2 * HEAD_DIM), f32), pltpu.SemaphoreType.DMA((3,))],
        compiler_params=params,
        cost_estimate=cost,
        name="last_block",
    )(info, starts, kv, qs, dos, rows, own_dq, own_dkv, dkv, dq12)

    def returns(mask, dq3, send, far, own):
        pairs = [(i, i ^ half_axis) for i in range(2 * half_axis) if mask >> (i % half_axis * GROUPS // half_axis) & 1]
        theirs3 = lax.ppermute(dq3, "seq", pairs) if pairs else dq3
        odd = lax.axis_index("seq") % 2 == 1
        halves = jnp.concatenate([send[:window], far], axis=1)
        third, second, first = (halves[n * tokens : (n + 1) * tokens] for n in range(BACK))
        mate = swapped(jnp.concatenate([jnp.where(odd, third, first), first], axis=0), "seq", 1).astype(f32)
        second = second.astype(f32) + mate[:tokens]
        mine = jnp.where(odd, 0.0, mate[tokens:])
        own = own + mine[:, HEAD_DIM:]
        sent = send[window:].astype(f32) + mine[:, :HEAD_DIM]
        arrived = swapped(jnp.concatenate([second[:, :HEAD_DIM].astype(bf16), sent.astype(bf16), send[:tokens]], axis=0),
                          "head", 1).astype(f32)
        back3 = lax.ppermute((far[:tokens].astype(f32) + arrived[2 * tokens :]).astype(bf16), "seq",
                             [(i, i - 3) for i in range(4, devices, 2)])
        back2 = shifted((second[:, HEAD_DIM:] + arrived[:tokens]).astype(bf16), "seq", -2)
        return (theirs3, own + arrived[tokens : 2 * tokens], back2, back3)

    branches = [functools.partial(returns, mask) for mask in range(1 << GROUPS)]
    theirs3, own, back2, back3 = lax.switch(branch.reshape(()), branches, dq3, send, far, own)

    grad_half = jax.ShapeDtypeStruct((HEAD_DIM // 2, tokens), bf16)
    whole = jax.ShapeDtypeStruct((tokens, feature), bf16)
    query_grad, key_grad, value_grad = pl.pallas_call(
        finish_kernel,
        in_specs=[smem, vmem, anywhere, vmem] + [anywhere] * 2 + [hbm],
        out_specs=[hbm, hbm, hbm],
        out_shape=[whole, grad_half, grad_half],
        input_output_aliases={6: 0},
        scratch_shapes=[pltpu.SemaphoreType.DMA((9,)), pltpu.VMEM((BLOCK, feature), bf16)]
        + [pltpu.VMEM((tokens, HEAD_DIM), bf16)] * 2 + [pltpu.VMEM((HEAD_DIM // 2, tokens), bf16)] * 2,
        compiler_params=params,
        name="place_blocks",
    )(info, theirs12, theirs3, own, back2, back3, placed)
    return query_grad, key_grad.T, value_grad.T


def solution(mesh):
    placed = (
        P("seq", "head"),
        P("seq", None),
        P("seq", None),
        P("seq", "head"),
        P("seq", "head"),
        P("head", "seq"),
        P(),
        P(),
    )
    return jax.shard_map(
        on_device,
        mesh=mesh,
        in_specs=placed,
        out_specs=(P("seq", "head"), P("seq", "head"), P("seq", "head")),
        check_vma=False,
    )
```

```python
import functools

import jax
import jax.numpy as jnp
from jax import lax
from jax.experimental import pallas as pl
from jax.experimental.pallas import tpu as pltpu
from jax.sharding import PartitionSpec as P

HEAD_DIM = 128
BLOCK = 128
BACK = 3
VMEM_LIMIT = 20 * 2**20
GROUPS = 4
LOG2E = 1.4426950408889634
SCALE = HEAD_DIM ** -0.5


def shifted(value, axis, steps):
    count = lax.axis_size(axis)
    first, last = (max(0, -steps), min(count, count - steps))
    return lax.ppermute(value, axis, [(i, i + steps) for i in range(first, last)])


def swapped(array, axis, apart):
    return lax.ppermute(array, axis, [(i, i ^ apart) for i in range(lax.axis_size(axis))])


def dot(a, b):
    return jnp.dot(a, b, preferred_element_type=jnp.float32)


def dot_nt(a, b):
    return lax.dot_general(a, b, (((1,), (1,)), ((), ())), preferred_element_type=jnp.float32)


def tile_grads(kt, vt, qs, dos, rows, allowed, heads):
    scores = dot_nt(kt, qs)
    prob_grad = dot_nt(vt, dos)
    weights, score_grads = [], []
    for h in range(heads):
        cols = slice(h * BLOCK, (h + 1) * BLOCK)
        lse = rows[h : h + 1, :]
        delta = rows[heads + h : heads + h + 1, :]
        w = jnp.where(allowed, jnp.exp2(scores[:, cols] * (SCALE * LOG2E) - lse), 0.0)
        weights.append(w.astype(jnp.bfloat16))
        score_grads.append((w * (prob_grad[:, cols] - delta)).astype(jnp.bfloat16))
    w_half = jnp.concatenate(weights, axis=1)
    s_grad = jnp.concatenate(score_grads, axis=1)
    dv = dot(w_half, dos)
    dk = dot(s_grad, qs)
    dq_t = dot(kt.T, s_grad)
    return dq_t, dk, dv


def plan_info(info_ref, branch_ref, lengths_ref, plan_ref, device, half_axis, side, per_device):
    first = device * per_device
    partner = device ^ half_axis
    locals_ = range(per_device)
    theirs = [plan_ref[partner * per_device + s] for s in locals_]
    mine = [plan_ref[first + s] for s in locals_]
    ranks = []
    for l in locals_:
        rank = per_device + l
        for s in locals_:
            rank = jnp.where(theirs[s] == first + l, s, rank)
        ranks.append(rank)
    position = [sum((ranks[m] < ranks[l]).astype(jnp.int32) for m in locals_ if m != l) for l in locals_]
    starts = [jnp.int32(0)] * per_device
    begin = jnp.int32(0)
    for n in range(lengths_ref.shape[0]):
        starts = [jnp.where(begin <= (first + l) * BLOCK, begin, starts[l]) for l in locals_]
        begin = begin + lengths_ref[n]
    info_ref[0] = device
    info_ref[1] = side
    for i in locals_:
        info_ref[2 + i] = sum(jnp.where(position[l] == i, l, 0) for l in locals_)
        info_ref[5 + i] = sum(jnp.where(position[l] == i, starts[l], 0) for l in locals_)
    far_rank = jnp.int32(0)
    for s in locals_:
        local = mine[s] - first
        near = (local >= 0) & (local < per_device)
        near_position = sum(jnp.where(local == l, position[l], 0) for l in locals_)
        info_ref[8 + s] = jnp.where(near, near_position, per_device + far_rank)
        far_rank = far_rank + jnp.where(near, 0, 1)
    mask = jnp.int32(0)
    for pair in range(half_axis):
        full = jnp.bool_(True)
        for s in locals_:
            local = plan_ref[pair * per_device + s] - pair * per_device
            full = full & ((local < 0) | (local >= per_device))
        mask = mask | jnp.where(full, 1 << (pair * GROUPS // half_axis), 0)
    branch_ref[0] = mask


def prepare_kernel(heads, half_axis, lengths_ref, plan_ref, q_hbm, o_hbm, do_hbm, lse_ref,
                   rows_ref, starts_ref, qs_ref, dos_ref, info_ref, branch_ref, q_buf, o_buf, do_buf, sems):
    tokens = q_buf.shape[0]
    blocks = tokens // BLOCK
    feature = heads * HEAD_DIM

    def copies(j):
        rows = pl.ds(j * BLOCK, BLOCK)
        pairs = ((do_hbm, do_buf), (o_hbm, o_buf), (q_hbm, q_buf))
        return [pltpu.make_async_copy(a.at[rows, :], b.at[rows, :], sems.at[j, n]) for n, (a, b) in enumerate(pairs)]

    for j in range(blocks):
        for c in copies(j):
            c.start()
    device = lax.axis_index("seq")
    plan_info(info_ref, branch_ref, lengths_ref, plan_ref, device, half_axis, lax.axis_index("head") & 1, blocks)

    pos = device * tokens + lax.broadcasted_iota(jnp.int32, (1, tokens), 1)
    start = jnp.zeros((1, tokens), jnp.int32)
    begin = jnp.int32(0)
    for n in range(lengths_ref.shape[0]):
        start = jnp.where(pos >= begin, begin, start)
        begin = begin + lengths_ref[n]

    ones = jnp.ones((8, 2 * HEAD_DIM), jnp.bfloat16)
    for j in range(blocks):
        rows = pl.ds(j * BLOCK, BLOCK)
        lanes = slice(j * BLOCK, (j + 1) * BLOCK)
        starts_ref[j] = jnp.broadcast_to(start[:, lanes], (8, BLOCK))
        rows_ref[j, 0:heads, :] = lse_ref[:, lanes].astype(jnp.float32) * LOG2E
        for c in copies(j):
            c.wait()
        for h in range(heads):
            cols = pl.ds(h * HEAD_DIM, HEAD_DIM)
            stacked = pl.ds(j * feature + h * HEAD_DIM, HEAD_DIM)
            qs_ref[stacked, :] = q_buf[rows, cols]
            dos_ref[stacked, :] = do_buf[rows, cols]
            prod = do_buf[rows, cols].astype(jnp.float32) * o_buf[rows, cols].astype(jnp.float32)
            high = prod.astype(jnp.bfloat16)
            low = (prod - high.astype(jnp.float32)).astype(jnp.bfloat16)
            row = dot_nt(ones, jnp.concatenate([high, low], axis=1))
            rows_ref[j, heads + h : heads + h + 1, :] = row[0:1, :]


def own_kernel(heads, info, starts_ref, kv_ref, qs_ref, dos_ref, rows_ref, dq_ref, dkv_ref):
    tokens = kv_ref.shape[0]
    feature = heads * HEAD_DIM
    base = info[0] * tokens
    dkv_ref[...] = jnp.zeros_like(dkv_ref)
    for j in range(tokens // BLOCK):
        rows = pl.ds(j * BLOCK, BLOCK)
        keys = slice(0, (j + 1) * BLOCK)
        queries = pl.ds(j * feature, feature)
        pos_row = base + j * BLOCK + lax.broadcasted_iota(jnp.int32, (1, BLOCK), 1)
        key_pos = base + lax.broadcasted_iota(jnp.int32, ((j + 1) * BLOCK, BLOCK), 0)
        allowed = (key_pos >= starts_ref[j, 0:1, :]) & (key_pos <= pos_row)
        dq_t, dk, dv = tile_grads(kv_ref[keys, 0:HEAD_DIM], kv_ref[keys, HEAD_DIM : 2 * HEAD_DIM],
                                  qs_ref[queries, :], dos_ref[queries, :], rows_ref.at[j], allowed, heads)
        dq_ref[rows, :] = dq_t
        dkv_ref[keys, 0:HEAD_DIM] += dk
        dkv_ref[keys, HEAD_DIM : 2 * HEAD_DIM] += dv


def block_rest(i, heads, info, starts_ref, kv_ref, qs_ref, dos_ref, rows_ref, dqa_ref, dkv_ref, dq_ref, out_ref, row=0):
    tokens = dqa_ref.shape[0]
    feature = heads * HEAD_DIM
    blocks = tokens // BLOCK
    base = (info[0] - BACK) * tokens
    block = jnp.clip(info[2 + i], 0, blocks - 1)
    first = jnp.clip(lax.div(info[5 + i] - base, tokens), 0, BACK)
    queries = pl.ds(pl.multiple_of(block * feature, feature), feature)
    dq_ref[...] = dqa_ref[pl.ds(pl.multiple_of(block * BLOCK, BLOCK), BLOCK), :]
    start_row = starts_ref[block, 0:1, :]

    def step(t, carry):
        keys = pl.ds(pl.multiple_of(t * tokens, tokens), tokens)
        key_pos = base + t * tokens + lax.broadcasted_iota(jnp.int32, (tokens, BLOCK), 0)
        dq_t, dk, dv = tile_grads(kv_ref[keys, 0:HEAD_DIM], kv_ref[keys, HEAD_DIM : 2 * HEAD_DIM],
                                  qs_ref[queries, :], dos_ref[queries, :], rows_ref.at[block],
                                  key_pos >= start_row, heads)
        dq_ref[...] += dq_t
        dkv_ref[keys, 0:HEAD_DIM] += dk
        dkv_ref[keys, HEAD_DIM : 2 * HEAD_DIM] += dv
        return carry

    lax.fori_loop(first, BACK, step, 0)
    for h in range(heads):
        cols = pl.ds(h * HEAD_DIM, HEAD_DIM)
        out_ref[pl.ds(row, BLOCK), cols] = (dq_ref[:, cols].T * SCALE).astype(jnp.bfloat16)


def first_kernel(heads, info, starts_ref, mate_ref, chip_ref, far_ref, qs_ref, dos_ref, rows_ref, dqa_ref,
                 out_ref, kv_ref, dkv_ref, dq_ref):
    tokens = chip_ref.shape[0]
    dkv_ref[...] = jnp.zeros_like(dkv_ref)
    kv_ref[pl.ds(tokens, tokens), :] = chip_ref[...]
    odd = lax.rem(info[0], 2)
    for parity, (third_back, one_back) in enumerate(((far_ref, mate_ref), (mate_ref, far_ref))):
        @pl.when(odd == parity)
        def _(third_back=third_back, one_back=one_back):
            kv_ref[pl.ds(0, tokens), :] = third_back[...]
            kv_ref[pl.ds(2 * tokens, tokens), :] = one_back[...]

    for i in range(2):
        block_rest(i, heads, info, starts_ref, kv_ref, qs_ref, dos_ref, rows_ref, dqa_ref, dkv_ref, dq_ref, out_ref,
                   i * BLOCK)


def place(info, arrays, out_ref, sems, act):
    for s in range(3):
        for number, array in arrays:
            @pl.when(info[8 + s] == number)
            def _(array=array, s=s):
                getattr(pltpu.make_async_copy(array, out_ref.at[pl.ds(s * BLOCK, BLOCK), :], sems.at[s]), act)()


def both_blocks(first, pair):
    return [(first, pair.at[pl.ds(0, BLOCK), :]), (first + 1, pair.at[pl.ds(BLOCK, BLOCK), :])]


def rest_kernel(heads, info, starts_ref, kv_ref, qs_ref, dos_ref, rows_ref, dqa_ref, dkva_ref, dkvb_ref,
                mine12, third_ref, send_ref, far_ref, own_ref, placed_ref, dq_ref, dkv_ref, sems):
    tokens = dkva_ref.shape[0]
    place(info, both_blocks(0, mine12), placed_ref, sems, "start")
    dkv_ref[...] = dkvb_ref[...]
    block_rest(2, heads, info, starts_ref, kv_ref, qs_ref, dos_ref, rows_ref, dqa_ref, dkv_ref, dq_ref, third_ref)
    place(info, [(2, third_ref)], placed_ref, sems, "start")

    side = info[1]
    half = HEAD_DIM // 2
    left = lax.broadcasted_iota(jnp.int32, (tokens, HEAD_DIM), 1) < half
    for n in range(BACK + 1):
        rows = pl.ds(n * tokens, tokens)
        ref, first = (dkv_ref, n * tokens) if n < BACK else (dkva_ref, 0)
        dk = ref[pl.ds(first, tokens), 0:HEAD_DIM] * SCALE
        dv = ref[pl.ds(first, tokens), HEAD_DIM : 2 * HEAD_DIM]
        low = jnp.where(left, dk, pltpu.roll(dv, half, 1))
        high = jnp.where(left, pltpu.roll(dk, half, 1), dv)
        send_ref[rows, :] = jnp.where(side == 0, high, low).astype(jnp.bfloat16)
        kept = jnp.where(side == 0, low, high)
        if n < BACK:
            far_ref[rows, :] = kept.astype(jnp.bfloat16)
        else:
            own_ref[...] = kept
    place(info, both_blocks(0, mine12) + [(2, third_ref)], placed_ref, sems, "wait")


def finish_kernel(info, theirs12, theirs3_hbm, own_ref, placed_ref,
                  out_ref, key_hbm, value_hbm, sems, theirs3, key_ref, value_ref):
    place(info, both_blocks(3, theirs12), out_ref, sems, "start")
    has_third = (info[8] == 5) | (info[9] == 5) | (info[10] == 5)

    @pl.when(has_third)
    def _():
        load = pltpu.make_async_copy(theirs3_hbm, theirs3, sems.at[6])
        load.start()
        load.wait()
        place(info, [(5, theirs3)], out_ref, sems, "start")

    total = own_ref[...]
    half = HEAD_DIM // 2
    for n in range(total.shape[0] // BLOCK):
        lanes = slice(n * BLOCK, (n + 1) * BLOCK)
        turned = total[lanes, :].T.astype(jnp.bfloat16)
        key_ref[:, lanes] = turned[:half]
        value_ref[:, lanes] = turned[half:]
    stores = [pltpu.make_async_copy(a, b, sems.at[7 + n])
              for n, (a, b) in enumerate(((key_ref, key_hbm), (value_ref, value_hbm)))]
    for store in stores:
        store.start()
    place(info, both_blocks(3, theirs12) + [(5, theirs3)], out_ref, sems, "wait")
    for store in stores:
        store.wait()


def on_device(queries, key_states, value_states, attn_out, grad_out, log_norm, lengths, block_plan):
    tokens, feature = queries.shape
    heads = feature // HEAD_DIM
    blocks = tokens // BLOCK
    half_axis = lax.axis_size("seq") // 2
    window = BACK * tokens
    kv_group = lax.axis_index("head") // 2
    own_kv = jnp.concatenate([
        lax.dynamic_slice_in_dim(key_states, kv_group * HEAD_DIM, HEAD_DIM, 1),
        lax.dynamic_slice_in_dim(value_states, kv_group * HEAD_DIM, HEAD_DIM, 1)], axis=1)
    devices = 2 * half_axis
    chip_kv = shifted(own_kv, "seq", 2)
    far_kv = lax.ppermute(own_kv, "seq", [(i, i + 3 if i % 2 else i + 1) for i in range(devices) if i + 3 < devices or not i % 2])
    later = BACK * tokens
    f32, bf16, i32 = jnp.float32, jnp.bfloat16, jnp.int32
    queries, attn_out, grad_out, log_norm, lengths, block_plan = (
        pltpu.with_memory_space_constraint(a, pltpu.HBM)
        for a in (queries, attn_out, grad_out, log_norm, lengths, block_plan))
    smem = pl.BlockSpec(memory_space=pltpu.SMEM)
    vmem = pl.BlockSpec(memory_space=pltpu.VMEM)
    hbm = pl.BlockSpec(memory_space=pltpu.HBM)
    anywhere = pl.BlockSpec(memory_space=pl.ANY)
    params = pltpu.CompilerParams(vmem_limit_bytes=VMEM_LIMIT)
    cost = pl.CostEstimate(flops=1_000, bytes_accessed=1_000, transcendentals=0)
    rows, starts, qs, dos, info, branch = pl.pallas_call(
        functools.partial(prepare_kernel, heads, half_axis),
        in_specs=[smem, smem, hbm, hbm, hbm, vmem],
        out_specs=[vmem] * 4 + [smem] * 2,
        out_shape=[pltpu.VMEM((blocks, 16, BLOCK), f32),
                   pltpu.VMEM((blocks, 8, BLOCK), i32),
                   pltpu.VMEM((blocks * feature, HEAD_DIM), bf16),
                   pltpu.VMEM((blocks * feature, HEAD_DIM), bf16),
                   jax.ShapeDtypeStruct((16,), i32),
                   jax.ShapeDtypeStruct((1,), i32)],
        scratch_shapes=[pltpu.VMEM((tokens, feature), bf16)] * 3 + [pltpu.SemaphoreType.DMA((blocks, 3))],
        compiler_params=params,
        cost_estimate=cost,
        name="prepare",
    )(lengths, block_plan, queries, attn_out, grad_out, log_norm)

    chip_kv, rows = lax.optimization_barrier((chip_kv, rows))
    mate_kv = swapped(chip_kv, "seq", 1)
    own_dq, own_dkv = pl.pallas_call(
        functools.partial(own_kernel, heads),
        in_specs=[smem] + [vmem] * 5,
        out_specs=[vmem] * 2,
        out_shape=[pltpu.VMEM((tokens, feature), f32), pltpu.VMEM((tokens, 2 * HEAD_DIM), f32)],
        compiler_params=params,
        cost_estimate=cost,
        name="own_keys",
    )(info, starts, own_kv, qs, dos, rows)

    dq12, kv, dkv = pl.pallas_call(
        functools.partial(first_kernel, heads),
        in_specs=[smem] + [vmem] * 8,
        out_specs=[vmem] * 3,
        out_shape=[pltpu.VMEM((2 * BLOCK, feature), bf16),
                   pltpu.VMEM((later, 2 * HEAD_DIM), bf16),
                   pltpu.VMEM((later, 2 * HEAD_DIM), f32)],
        scratch_shapes=[pltpu.VMEM((BLOCK, feature), f32)],
        compiler_params=params,
        cost_estimate=cost,
        name="first_blocks",
    )(info, starts, mate_kv, chip_kv, far_kv, qs, dos, rows, own_dq)
    theirs12 = swapped(dq12, "seq", half_axis)

    dq3, send, far, own, placed = pl.pallas_call(
        functools.partial(rest_kernel, heads),
        in_specs=[smem] + [vmem] * 9,
        out_specs=[vmem] * 4 + [hbm],
        out_shape=[pltpu.VMEM((BLOCK, feature), bf16),
                   pltpu.VMEM((window + tokens, HEAD_DIM), bf16),
                   pltpu.VMEM((window, HEAD_DIM), bf16),
                   pltpu.VMEM((tokens, HEAD_DIM), f32),
                   jax.ShapeDtypeStruct((tokens, feature), bf16)],
        scratch_shapes=[pltpu.VMEM((BLOCK, feature), f32), pltpu.VMEM((later, 2 * HEAD_DIM), f32), pltpu.SemaphoreType.DMA((3,))],
        compiler_params=params,
        cost_estimate=cost,
        name="last_block",
    )(info, starts, kv, qs, dos, rows, own_dq, own_dkv, dkv, dq12)

    def returns(mask, dq3, send, far, own):
        pairs = [(i, i ^ half_axis) for i in range(2 * half_axis) if mask >> (i % half_axis * GROUPS // half_axis) & 1]
        theirs3 = lax.ppermute(dq3, "seq", pairs) if pairs else dq3
        odd = lax.axis_index("seq") % 2 == 1
        halves = jnp.concatenate([send[:window], far], axis=1)
        third, second, first = (halves[n * tokens : (n + 1) * tokens] for n in range(BACK))
        mate = swapped(jnp.concatenate([jnp.where(odd, third, first), first], axis=0), "seq", 1).astype(f32)
        second = second.astype(f32) + mate[:tokens]
        mine = jnp.where(odd, 0.0, mate[tokens:])
        own = own + mine[:, HEAD_DIM:]
        sent = send[window:].astype(f32) + mine[:, :HEAD_DIM]
        arrived = swapped(jnp.concatenate([second[:, :HEAD_DIM].astype(bf16), sent.astype(bf16), send[:tokens]], axis=0),
                          "head", 1).astype(f32)
        back3 = lax.ppermute((far[:tokens].astype(f32) + arrived[2 * tokens :]).astype(bf16), "seq",
                             [(i, i - 3) for i in range(4, devices, 2)])
        back2 = shifted((second[:, HEAD_DIM:] + arrived[:tokens]).astype(bf16), "seq", -2)
        return theirs3, own + arrived[tokens : 2 * tokens] + back2.astype(f32) + back3.astype(f32)

    branches = [functools.partial(returns, mask) for mask in range(1 << GROUPS)]
    theirs3, own = lax.switch(branch.reshape(()), branches, dq3, send, far, own)

    grad_half = jax.ShapeDtypeStruct((HEAD_DIM // 2, tokens), bf16)
    whole = jax.ShapeDtypeStruct((tokens, feature), bf16)
    query_grad, key_grad, value_grad = pl.pallas_call(
        finish_kernel,
        in_specs=[smem, vmem, anywhere, vmem, hbm],
        out_specs=[hbm, hbm, hbm],
        out_shape=[whole, grad_half, grad_half],
        input_output_aliases={4: 0},
        scratch_shapes=[pltpu.SemaphoreType.DMA((9,)), pltpu.VMEM((BLOCK, feature), bf16)]
        + [pltpu.VMEM((HEAD_DIM // 2, tokens), bf16)] * 2,
        compiler_params=params,
        name="place_blocks",
    )(info, theirs12, theirs3, own, placed)
    return query_grad, key_grad.T, value_grad.T


def solution(mesh):
    placed = (
        P("seq", "head"),
        P("seq", None),
        P("seq", None),
        P("seq", "head"),
        P("seq", "head"),
        P("head", "seq"),
        P(),
        P(),
    )
    return jax.shard_map(
        on_device,
        mesh=mesh,
        in_specs=placed,
        out_specs=(P("seq", "head"), P("seq", "head"), P("seq", "head")),
        check_vma=False,
    )
```
